32 devices in a mesh: group: 2 (over y), seq: 8 (over z, x), head: 2 (over core).
Axes of the slice: x: 2, y: 2, z: 4, core: 2. Of those that a mesh axis runs over, the one named last changes fastest.
Arguments:
- response_query: bfloat16 [16, 128, 4096], P('group', 'seq', 'head'), parts along dimension 0, may hold values from -6 to 6, as said below
- response_key: bfloat16 [16, 128, 512], P('group', 'seq', 'head'), parts along dimension 0, may hold values from -8 to 8, as said below
- response_value: bfloat16 [16, 128, 512], P('group', 'seq', 'head'), parts along dimension 0, may hold values from -6 to 6
- response_grad: bfloat16 [16, 128, 4096], P('group', 'seq', 'head'), parts along dimension 0, may hold values from -6 to 6
- prompt_key: bfloat16 [192, 512], P(('group', 'seq'), 'head'), parts along dimension 0, may hold values from -8 to 8, as said below
- prompt_value: bfloat16 [192, 512], P(('group', 'seq'), 'head'), parts along dimension 0, may hold values from -6 to 6
- lengths: int32 [16], P('group'), parts along dimension 0, may hold values from 1 to 128, 512 in all
- home_rank: int32 [16], P('group'), parts along dimension 0, may hold values from 0 to 7, each once
- prompt_seen: int32 [16], P('group'), parts along dimension 0, may hold values from 24 to 96
Outputs:
- response_output: bfloat16 [16, 128, 4096], P(('group', 'seq'), None, 'head'), parts along dimension 0
- response_query_grad: bfloat16 [16, 128, 4096], P('group', 'seq', 'head'), parts along dimension 0
- response_key_grad: bfloat16 [16, 128, 512], P('group', 'seq', 'head'), parts along dimension 0
- response_value_grad: bfloat16 [16, 128, 512], P('group', 'seq', 'head'), parts along dimension 0
- prompt_key_grad: bfloat16 [192, 512], P(('group', 'seq'), 'head'), parts along dimension 0
- prompt_value_grad: bfloat16 [192, 512], P(('group', 'seq'), 'head'), parts along dimension 0
The draws below stay inside these ranges and needn't reach their ends.
There are 2 independent parts, one for each index of `group`. The reference program is written for one: setup_inputs(seed, part) draws one part's arguments, and reference() takes and returns one part's arrays. A program takes and returns all parts, laid end to end along the dimension named above; each array names one. Nothing has to cross between parts.
Inputs may be any that keep to these rules, and one draw needn't show every extreme that they name: `response_query`: queries are finite. `response_key`: keys are finite. `prompt_key`: keys are finite. `lengths`: some response has exactly 128 tokens. `home_rank`: every index of seq is the home of exactly one response.
All inputs are finite; a program needn't handle non-finite values.
Results may differ from the reference program's by a relative error of at most 0.017.
The reference program's roundings to bfloat16 on the way (of `weights` and `dlogit`) count: a program that leaves them out, or rounds other values in their place, can miss the bound.
Values may be sent and summed in bfloat16 or wider, within the bound.
A program may use at most 128 MiB of HBM per device.

```python
import math
import jax
import jax.numpy as jnp
import numpy as np
from jax import lax

QHEADS = 32
KVHEADS = 4
HEAD_DIM = 128
MAX_LEN = 128
RESPONSES = 8
PROMPT = 96


def query_rows(key, salt, shape):
    own_key = jax.random.fold_in(key, salt)
    base = jnp.clip(jax.random.normal(jax.random.fold_in(own_key, 1), shape, jnp.float32), -6.0, 6.0)
    return base


def key_rows(key, salt, shape):
    own_key = jax.random.fold_in(key, salt)
    base = jnp.clip(jax.random.normal(jax.random.fold_in(own_key, 1), shape, jnp.float32), -6.0, 6.0)
    return base


def draw_response_query(key, part):
    return query_rows(key, 11, (RESPONSES, MAX_LEN, QHEADS * HEAD_DIM)).astype(jnp.bfloat16)


def draw_response_key(key, part):
    return key_rows(key, 13, (RESPONSES, MAX_LEN, KVHEADS * HEAD_DIM)).astype(jnp.bfloat16)


def draw_prompt_key(key, part):
    return key_rows(key, 14, (PROMPT, KVHEADS * HEAD_DIM)).astype(jnp.bfloat16)


def touch_ends(drawn, key, low, top_value):
    extent = drawn.shape
    spot = [jax.random.randint(jax.random.fold_in(key, axis), (), 0, extent[axis]) for axis in range(len(extent))]
    drawn = drawn.at[tuple(spot)].set(low)
    longest = extent.index(max(extent))
    spot[longest] = (spot[longest] + 1) % extent[longest]
    return drawn.at[tuple(spot)].set(top_value)


def block_levels(key, dims, pieces, smallest, largest):
    level = 1.0
    for dim, blocks in pieces:
        steps = jax.random.uniform(jax.random.fold_in(jax.random.fold_in(key, 6), dim), (blocks,), jnp.float32, smallest / len(pieces), largest / len(pieces))
        level = level * jnp.repeat(jnp.exp(steps), dims[dim] // blocks).reshape((-1,) + (1,) * (len(dims) - 1 - dim))
    return level


def split_up(number_of, total, limit, slope):
    loads = [(1 << 20) // math.isqrt(grade ** slope) + 1 for grade in range(2, number_of + 1)]
    spare, holding = total - limit - (number_of - 1), [1] * (number_of - 1)
    while spare > 0:
        free = [i for i in range(number_of - 1) if holding[i] < limit]
        pool, remaining = sum([loads[i] for i in free]), spare
        for i in free:
            addition = min(limit - holding[i], max(1, remaining * loads[i] // pool), spare)
            holding[i] = holding[i] + addition
            spare = spare - addition
    return np.array([limit] + holding)


def ragged(rng, amount, total, most, slope):
    if amount == 2:
        one = jax.random.randint(rng, (), max(1, total - most), min(most, total - 1) + 1)
        return jnp.stack([one, total - one])
    tallies = jnp.asarray(split_up(amount, total, most, slope), jnp.int32)
    couples = (amount - 1) // 2
    source_of, taker = tallies[1:1 + 2 * couples:2], tallies[2:2 + 2 * couples:2]
    slack = jnp.minimum(source_of - 1, most - taker)
    passed = jax.random.randint(jax.random.fold_in(rng, 1), (couples,), 0, 1 << 20) % (slack + 1)
    tallies = tallies.at[1:1 + 2 * couples:2].set(source_of - passed).at[2:2 + 2 * couples:2].set(taker + passed)
    return tallies[jax.random.permutation(jax.random.fold_in(rng, 2), amount)]


def scatter_about(key, extent, scale, reach, shards=(), held_as=jnp.bfloat16):
    factor_of = block_levels(key, extent, shards, -0.22, 0.18) if shards else 1.0
    values = jax.random.normal(key, extent, jnp.float32) * scale * factor_of
    return jnp.minimum(jnp.maximum(values, -reach), reach).astype(held_as)


def setup_inputs(seed: int = 0, part: int = 0) -> dict:
    keys = jax.random.split(jax.random.key(seed), 10)
    part_splits = jax.random.split(jax.random.fold_in(keys[9], part), 10)
    return {
        "response_query": draw_response_query(jax.random.fold_in(jax.random.fold_in(keys[9], part), 71), part),
        "response_key": draw_response_key(jax.random.fold_in(jax.random.fold_in(keys[9], part), 71), part),
        "response_value": scatter_about(part_splits[2], (RESPONSES, MAX_LEN, KVHEADS * HEAD_DIM), 1.0, 6.0, ((1, 8), (2, 2))),
        "response_grad": scatter_about(part_splits[3], (RESPONSES, MAX_LEN, QHEADS * HEAD_DIM), 1.0, 6.0, ((1, 8), (2, 2))),
        "prompt_key": draw_prompt_key(jax.random.fold_in(jax.random.fold_in(keys[9], part), 71), part),
        "prompt_value": scatter_about(part_splits[5], (PROMPT, KVHEADS * HEAD_DIM), 1.0, 6.0, ((0, 8), (1, 2))),
        "lengths": ragged(part_splits[6], RESPONSES, RESPONSES * MAX_LEN // 2, MAX_LEN, 2).astype(jnp.int32),
        "home_rank": jax.random.permutation(part_splits[7], RESPONSES).astype(jnp.int32),
        "prompt_seen": touch_ends(jax.random.randint(part_splits[8], (RESPONSES,), PROMPT // 4, PROMPT + 1), jax.random.fold_in(part_splits[8], 1), PROMPT // 4, PROMPT).astype(jnp.int32),
    }


NEG_FILL = -1.0e30


def attend(queries, all_keys, all_values, grad_rows, allowed, live_rows, scale_factor):
    row_count = queries.shape[0]
    kv_count = all_keys.shape[1] // HEAD_DIM
    group_size = queries.shape[1] // all_keys.shape[1]
    outputs = []
    query_grads = []
    key_grads = []
    value_grads = []
    for head_index in range(kv_count):
        low = head_index * group_size * HEAD_DIM
        high = (head_index + 1) * group_size * HEAD_DIM
        query_head = queries[:, low:high].reshape(row_count, group_size, HEAD_DIM).astype(jnp.float32)
        key_head = all_keys[:, head_index * HEAD_DIM:(head_index + 1) * HEAD_DIM].astype(jnp.float32)
        value_head = all_values[:, head_index * HEAD_DIM:(head_index + 1) * HEAD_DIM].astype(jnp.float32)
        grad_head = jnp.where(live_rows[:, None], grad_rows[:, low:high], jnp.zeros((), jnp.bfloat16))
        grad_head = grad_head.reshape(row_count, group_size, HEAD_DIM).astype(jnp.float32)
        logits = jnp.einsum("rhd,kd->rhk", query_head, key_head) * scale_factor
        logits = jnp.where(allowed[:, None, :], logits, NEG_FILL)
        row_max = jnp.max(logits, axis=2, keepdims=True)
        log_total = row_max + jnp.log(jnp.sum(jnp.exp(logits - row_max), axis=2, keepdims=True))
        prob = jnp.exp(logits - log_total)
        weights = lax.optimization_barrier(prob.astype(jnp.bfloat16)).astype(jnp.float32)
        mixed = jnp.einsum("rhk,kd->rhd", weights, value_head)
        output_head = jnp.where(live_rows[:, None, None], mixed, 0.0).astype(jnp.bfloat16)
        output_wide = lax.optimization_barrier(output_head).astype(jnp.float32)
        row_dot = jnp.sum(grad_head * output_wide, axis=2, keepdims=True)
        spread = jnp.einsum("rhd,kd->rhk", grad_head, value_head)
        dlogit = lax.optimization_barrier((prob * (spread - row_dot)).astype(jnp.bfloat16)).astype(jnp.float32)
        query_grads.append((jnp.einsum("rhk,kd->rhd", dlogit, key_head) * scale_factor).reshape(row_count, group_size * HEAD_DIM))
        key_grads.append(jnp.einsum("rhk,rhd->kd", dlogit, query_head) * scale_factor)
        value_grads.append(jnp.einsum("rhk,rhd->kd", weights, grad_head))
        outputs.append(output_head.reshape(row_count, group_size * HEAD_DIM))
    return (jnp.concatenate(outputs, axis=1), jnp.concatenate(query_grads, axis=1),
            jnp.concatenate(key_grads, axis=1), jnp.concatenate(value_grads, axis=1))


def reference(response_query, response_key, response_value, response_grad, prompt_key,
              prompt_value, lengths, home_rank, prompt_seen):
    rank_count = home_rank.shape[0]
    rank_ids = jnp.arange(rank_count, dtype=jnp.int32)
    resident = jnp.sum(jnp.where(home_rank[None, :] == rank_ids[:, None], rank_ids[None, :], 0), axis=1).astype(jnp.int32)
    prompt_total = prompt_key.shape[0]
    max_length = response_query.shape[1]
    scale_factor = 1.0 / (HEAD_DIM ** 0.5)
    positions = jnp.arange(max_length, dtype=jnp.int32)
    prompt_cols = jnp.arange(prompt_total, dtype=jnp.int32)

    def one_response(carry, index):
        key_total, value_total = carry
        all_keys = jnp.concatenate([prompt_key, response_key[index]], axis=0)
        all_values = jnp.concatenate([prompt_value, response_value[index]], axis=0)
        seen_part = jnp.broadcast_to(prompt_cols[None, :] < prompt_seen[index], (max_length, prompt_total))
        causal_part = positions[None, :] <= positions[:, None]
        allowed = jnp.concatenate([seen_part, causal_part], axis=1)
        live_rows = positions < lengths[index]
        output, query_grad, key_grad, value_grad = attend(response_query[index], all_keys, all_values,
                                                          response_grad[index], allowed, live_rows, scale_factor)
        carry = (key_total + key_grad[:prompt_total], value_total + value_grad[:prompt_total])
        return carry, (output, query_grad.astype(jnp.bfloat16), key_grad[prompt_total:].astype(jnp.bfloat16),
                       value_grad[prompt_total:].astype(jnp.bfloat16))

    start = (jnp.zeros(prompt_key.shape, jnp.float32), jnp.zeros(prompt_value.shape, jnp.float32))
    (key_total, value_total), stacked = lax.scan(one_response, start, rank_ids)
    outputs, query_grads, key_grads, value_grads = stacked
    return (outputs[resident], query_grads, key_grads, value_grads,
            key_total.astype(jnp.bfloat16), value_total.astype(jnp.bfloat16))
```

```python
import functools

import jax
import jax.numpy as jnp
from jax import lax
from jax.experimental import pallas as pl
from jax.experimental.pallas import tpu as pltpu
from jax.sharding import PartitionSpec as P

HEAD_DIM = 128


NEG_FILL = -1e30


def head_logits(queries, all_keys, allowed, head_index, group_size, scale_factor):
    row_count = queries.shape[0]
    low = head_index * group_size * HEAD_DIM
    high = (head_index + 1) * group_size * HEAD_DIM
    query_head = queries[:, low:high].reshape(row_count, group_size, HEAD_DIM)
    key_head = all_keys[:, head_index * HEAD_DIM : (head_index + 1) * HEAD_DIM]
    logits = (
        jnp.einsum("rhd,kd->rhk", query_head, key_head, preferred_element_type=jnp.float32)
        * scale_factor
    )
    return (query_head, key_head, jnp.where(allowed[:, None, :], logits, NEG_FILL))


def forward(queries, all_keys, all_values, allowed, live_rows, scale_factor):
    row_count = queries.shape[0]
    kv_count = all_keys.shape[1] // HEAD_DIM
    group_size = queries.shape[1] // all_keys.shape[1]
    outputs = []
    totals = []
    for head_index in range(kv_count):
        query_head, key_head, logits = head_logits(
            queries, all_keys, allowed, head_index, group_size, scale_factor
        )
        value_head = all_values[:, head_index * HEAD_DIM : (head_index + 1) * HEAD_DIM]
        row_max = jnp.max(logits, axis=2, keepdims=True)
        log_total = row_max + jnp.log(jnp.sum(jnp.exp(logits - row_max), axis=2, keepdims=True))
        weights = jnp.exp(logits - log_total).astype(jnp.bfloat16)
        mixed = jnp.einsum("rhk,kd->rhd", weights, value_head, preferred_element_type=jnp.float32)
        output_head = jnp.where(live_rows[:, None, None], mixed, 0.0).astype(jnp.bfloat16)
        outputs.append(output_head.reshape(row_count, group_size * HEAD_DIM))
        totals.append(log_total)
    return (jnp.concatenate(outputs, axis=1), totals)


def head_terms(grad_rows, live_rows, output, head_index, group_size):
    row_count = grad_rows.shape[0]
    low = head_index * group_size * HEAD_DIM
    high = (head_index + 1) * group_size * HEAD_DIM
    grad_head = jnp.where(live_rows[:, None], grad_rows[:, low:high], jnp.zeros((), jnp.bfloat16))
    grad_head = grad_head.reshape(row_count, group_size, HEAD_DIM)
    output_head = lax.optimization_barrier(output[:, low:high]).reshape(
        row_count, group_size, HEAD_DIM
    )
    row_dot = jnp.sum(
        grad_head.astype(jnp.float32) * output_head.astype(jnp.float32), axis=2, keepdims=True
    )
    return (grad_head, row_dot)


def backward(
    queries, all_keys, all_values, grad_rows, allowed, live_rows, output, totals, scale_factor
):
    row_count = queries.shape[0]
    kv_count = all_keys.shape[1] // HEAD_DIM
    group_size = queries.shape[1] // all_keys.shape[1]
    query_grads = []
    key_grads = []
    value_grads = []
    for head_index in range(kv_count):
        query_head, key_head, logits = head_logits(
            queries, all_keys, allowed, head_index, group_size, scale_factor
        )
        value_head = all_values[:, head_index * HEAD_DIM : (head_index + 1) * HEAD_DIM]
        prob = jnp.exp(logits - totals[head_index])
        weights = prob.astype(jnp.bfloat16)
        grad_head, row_dot = head_terms(grad_rows, live_rows, output, head_index, group_size)
        spread = jnp.einsum(
            "rhd,kd->rhk", grad_head, value_head, preferred_element_type=jnp.float32
        )
        dlogit = (prob * (spread - row_dot)).astype(jnp.bfloat16)
        query_part = (
            jnp.einsum("rhk,kd->rhd", dlogit, key_head, preferred_element_type=jnp.float32)
            * scale_factor
        )
        query_grads.append(query_part.reshape(row_count, group_size * HEAD_DIM))
        key_grads.append(
            jnp.einsum("rhk,rhd->kd", dlogit, query_head, preferred_element_type=jnp.float32)
            * scale_factor
        )
        value_grads.append(
            jnp.einsum("rhk,rhd->kd", weights, grad_head, preferred_element_type=jnp.float32)
        )
    return (
        jnp.concatenate(query_grads, axis=1),
        jnp.concatenate(key_grads, axis=1),
        jnp.concatenate(value_grads, axis=1),
    )


def collective_body(
    response_query,
    response_key,
    response_value,
    response_grad,
    prompt_key,
    prompt_value,
    lengths,
    home_rank,
    prompt_seen,
):
    rank_count = home_rank.shape[0]
    rank_ids = jnp.arange(rank_count, dtype=jnp.int32)
    resident = jnp.sum(
        jnp.where(home_rank[None, :] == rank_ids[:, None], rank_ids[None, :], 0), axis=1
    )
    own_rank = lax.axis_index("seq")
    scale_factor = 1.0 / HEAD_DIM**0.5
    arrived = (
        lax.all_to_all(response_query[resident], "seq", split_axis=0, concat_axis=1, tiled=True),
        lax.all_to_all(response_key[resident], "seq", split_axis=0, concat_axis=1, tiled=True),
        lax.all_to_all(response_value[resident], "seq", split_axis=0, concat_axis=1, tiled=True),
        lax.all_to_all(response_grad[resident], "seq", split_axis=0, concat_axis=1, tiled=True),
    )
    queries = arrived[0][0]
    own_keys = arrived[1][0]
    own_values = arrived[2][0]
    grad_rows = arrived[3][0]
    own_response = resident[own_rank]
    length = lengths[own_response]
    visible = prompt_seen[own_response]
    max_length = queries.shape[0]
    prompt_rows = prompt_key.shape[0]
    prompt_total = prompt_rows * lax.axis_size("seq")
    positions = jnp.arange(max_length, dtype=jnp.int32)
    prompt_cols = jnp.arange(prompt_total, dtype=jnp.int32)
    seen_part = jnp.broadcast_to(prompt_cols[None, :] < visible, (max_length, prompt_total))
    allowed = jnp.concatenate([seen_part, positions[None, :] <= positions[:, None]], axis=1)
    live_rows = positions < length
    gathered_keys, gathered_values = (
        lax.all_gather(prompt_key, "seq", axis=0, tiled=True),
        lax.all_gather(prompt_value, "seq", axis=0, tiled=True),
    )
    all_keys = jnp.concatenate([gathered_keys, own_keys], axis=0)
    all_values = jnp.concatenate([gathered_values, own_values], axis=0)
    response_out, response_totals = forward(
        queries, all_keys, all_values, allowed, live_rows, scale_factor
    )
    query_grad, key_grad, value_grad = backward(
        queries,
        all_keys,
        all_values,
        grad_rows,
        allowed,
        live_rows,
        response_out,
        response_totals,
        scale_factor,
    )
    key_summed, value_summed = (
        lax.psum_scatter(key_grad[:prompt_total], "seq", scatter_dimension=0, tiled=True),
        lax.psum_scatter(value_grad[:prompt_total], "seq", scatter_dimension=0, tiled=True),
    )
    returned = (
        lax.all_to_all(
            query_grad.astype(jnp.bfloat16)[None], "seq", split_axis=1, concat_axis=0, tiled=True
        ),
        lax.all_to_all(
            key_grad[prompt_total:].astype(jnp.bfloat16)[None],
            "seq",
            split_axis=1,
            concat_axis=0,
            tiled=True,
        ),
        lax.all_to_all(
            value_grad[prompt_total:].astype(jnp.bfloat16)[None],
            "seq",
            split_axis=1,
            concat_axis=0,
            tiled=True,
        ),
    )
    return (
        response_out[None],
        returned[0][home_rank],
        returned[1][home_rank],
        returned[2][home_rank],
        key_summed.astype(jnp.bfloat16),
        value_summed.astype(jnp.bfloat16),
    )


ROW_TILE = 16
MESH = pl.DeviceIdType.MESH


def dot_last(left, right):
    return lax.dot_general(left, right, (((1,), (1,)), ((), ())), preferred_element_type=jnp.float32)


def dot_first(left, right):
    return lax.dot_general(left, right, (((0,), (0,)), ((), ())), preferred_element_type=jnp.float32)


def dot_plain(left, right):
    return lax.dot_general(left, right, (((1,), (0,)), ((), ())), preferred_element_type=jnp.float32)


def wait_bytes(ref, sem):
    pltpu.make_async_copy(ref, ref, sem).wait()


def kernel(
    n, pieces, prompt_rows,
    q_ref, k_ref, v_ref, g_ref, pk_ref, pv_ref, len_ref, home_ref, seen_ref,
    out_ref, dq_ref, dk_ref, dv_ref, dpk_ref, dpv_ref,
    send_qg, send_kv, in_qg, in_kv, grad_q, grad_kv, back_q, back_kv, acc,
    sem_send, sem_kv, sem_qg, sem_back,
):
    me = lax.axis_index("seq")
    rows = q_ref.shape[1]
    width = q_ref.shape[2]
    kv_width = k_ref.shape[2]
    kv_heads = kv_width // HEAD_DIM
    heads = width // HEAD_DIM
    group = heads // kv_heads
    total = n * rows
    slot = in_kv.shape[1] // n
    scale = 1.0 / HEAD_DIM**0.5

    barrier = pltpu.get_barrier_semaphore()
    for step in range(1, n):
        pl.semaphore_signal(
            barrier, inc=1, device_id={"seq": lax.rem(me + step, n)}, device_id_type=MESH
        )

    def resident(rank):
        found = jnp.int32(0)
        for r in range(n):
            found = jnp.where(home_ref[r] == rank, jnp.int32(r), found)
        return found

    def pair_cols(head):
        return head * 2 * HEAD_DIM, head * 2 * HEAD_DIM + HEAD_DIM

    prompt_pad = jnp.zeros((slot - prompt_rows, HEAD_DIM), jnp.float32)
    for rank in range(n):
        source = resident(rank)
        send_qg[rank, 0] = q_ref[source]
        send_qg[rank, 1] = g_ref[source]
        key_rows = k_ref[source]
        value_rows = v_ref[source]
        for h in range(kv_heads):
            kc, vc = pair_cols(h)
            own = slice(h * HEAD_DIM, (h + 1) * HEAD_DIM)
            send_kv[rank, 0, :, kc : kc + HEAD_DIM] = key_rows[:, own]
            send_kv[rank, 0, :, vc : vc + HEAD_DIM] = value_rows[:, own]
            for ref, col in ((pk_ref, kc), (pv_ref, vc)):
                part = ref[:, own].astype(jnp.float32)
                if slot > prompt_rows:
                    part = jnp.concatenate([part, prompt_pad], axis=0)
                send_kv[rank, 1, :, col : col + HEAD_DIM] = part.astype(jnp.bfloat16)

    pl.semaphore_wait(barrier, n - 1)

    own_rows = pl.ds(pl.multiple_of(me * rows, rows), rows)
    own_slots = pl.ds(pl.multiple_of(me * slot, slot), slot)
    piece_width = width // pieces
    for step in range(1, n):
        peer = lax.rem(me + step, n)
        pltpu.make_async_remote_copy(
            src_ref=send_kv.at[peer], dst_ref=in_kv.at[:, own_slots, :],
            send_sem=sem_send.at[0], recv_sem=sem_kv,
            device_id={"seq": peer}, device_id_type=MESH,
        ).start()
    for piece in range(pieces):
        cols = pl.ds(piece * piece_width, piece_width)
        for step in range(1, n):
            peer = lax.rem(me + step, n)
            pltpu.make_async_remote_copy(
                src_ref=send_qg.at[peer, :, :, cols], dst_ref=in_qg.at[:, own_rows, cols],
                send_sem=sem_send.at[1], recv_sem=sem_qg.at[piece],
                device_id={"seq": peer}, device_id_type=MESH,
            ).start()
    in_kv[:, own_slots, :] = send_kv[me]
    in_qg[:, own_rows, :] = send_qg[me]

    own = resident(me)
    length = len_ref[own]
    visible = seen_ref[own]
    keys_total = total + n * slot
    row_id = lax.broadcasted_iota(jnp.int32, (total, keys_total), 0)
    col_id = lax.broadcasted_iota(jnp.int32, (total, keys_total), 1)
    in_prompt = col_id - total
    prompt_slot = in_prompt // slot
    prompt_row = in_prompt - prompt_slot * slot
    prompt_id = prompt_slot * prompt_rows + prompt_row
    allowed = jnp.where(
        col_id < total,
        (col_id <= row_id).astype(jnp.int32),
        ((prompt_row < prompt_rows) & (prompt_id < visible)).astype(jnp.int32),
    ) > 0
    live = lax.broadcasted_iota(jnp.int32, (total, HEAD_DIM), 0) < length

    wait_bytes(in_kv.at[:, 0 : (n - 1) * slot, :], sem_kv)
    per_piece = heads // pieces
    pieces_per_kv = group // per_piece
    for piece in range(pieces):
        cols = pl.ds(piece * piece_width, piece_width)
        h = piece // pieces_per_kv
        kc, vc = pair_cols(h)
        keys = in_kv[:, :, kc : kc + HEAD_DIM].reshape(keys_total, HEAD_DIM)
        values = in_kv[:, :, vc : vc + HEAD_DIM].reshape(keys_total, HEAD_DIM)
        wait_bytes(in_qg.at[:, 0 : (n - 1) * rows, cols], sem_qg.at[piece])
        for a in range(per_piece):
            low = piece * piece_width + a * HEAD_DIM
            head_cols = slice(low, low + HEAD_DIM)
            query = in_qg[0, :, head_cols]
            grad_wide = jnp.where(live, in_qg[1, :, head_cols].astype(jnp.float32), 0.0)
            grad = grad_wide.astype(jnp.bfloat16)
            logits = jnp.where(allowed, dot_last(query, keys) * scale, NEG_FILL)
            exped = jnp.exp(logits - jnp.max(logits, axis=1, keepdims=True))
            prob = exped * (1.0 / jnp.sum(exped, axis=1, keepdims=True))
            weights = prob.astype(jnp.bfloat16)
            output = jnp.where(live, dot_plain(weights, values), 0.0).astype(jnp.bfloat16)
            out_ref[0, :, head_cols] = output
            row_dot = jnp.sum(grad_wide * output.astype(jnp.float32), axis=1, keepdims=True)
            dlogit = (prob * (dot_last(grad, values) - row_dot)).astype(jnp.bfloat16)
            grad_q[:, head_cols] = (dot_plain(dlogit, keys) * scale).astype(jnp.bfloat16)
            dkey = dot_first(dlogit, query)
            dvalue = dot_first(weights, grad)
            if piece % pieces_per_kv == 0 and a == 0:
                acc[0] = dkey
                acc[1] = dvalue
            else:
                acc[0] += dkey
                acc[1] += dvalue
        for step in range(1, n):
            peer = lax.rem(me + step, n)
            pltpu.make_async_remote_copy(
                src_ref=grad_q.at[pl.ds(pl.multiple_of(peer * rows, rows), rows), cols],
                dst_ref=back_q.at[me, :, cols],
                send_sem=sem_send.at[2], recv_sem=sem_back.at[0],
                device_id={"seq": peer}, device_id_type=MESH,
            ).start()
        if piece % pieces_per_kv == pieces_per_kv - 1:
            dkey = (acc[0] * scale).astype(jnp.bfloat16)
            dvalue = acc[1].astype(jnp.bfloat16)
            for col, part in ((kc, dkey), (vc, dvalue)):
                grad_kv[0, :, col : col + HEAD_DIM] = part[:total]
                grad_kv[1, :, col : col + HEAD_DIM] = part[total:]
            pair = pl.ds(kc, 2 * HEAD_DIM)
            for step in range(1, n):
                peer = lax.rem(me + step, n)
                pltpu.make_async_remote_copy(
                    src_ref=grad_kv.at[:, pl.ds(pl.multiple_of(peer * slot, slot), slot), pair],
                    dst_ref=back_kv.at[me, :, :, pair],
                    send_sem=sem_send.at[3], recv_sem=sem_back.at[1],
                    device_id={"seq": peer}, device_id_type=MESH,
                ).start()
    back_q[me] = grad_q[own_rows, :]
    back_kv[me] = grad_kv[:, own_slots, :]

    wait_bytes(back_q.at[0 : n - 1], sem_back.at[0])
    for r in range(n):
        dq_ref[r] = back_q[home_ref[r]]
    wait_bytes(back_kv.at[0 : n - 1], sem_back.at[1])
    for r in range(n):
        home = home_ref[r]
        pair_grad = back_kv[home, 0]
        for h in range(kv_heads):
            kc, vc = pair_cols(h)
            own = slice(h * HEAD_DIM, (h + 1) * HEAD_DIM)
            dk_ref[r, :, own] = pair_grad[:, kc : kc + HEAD_DIM]
            dv_ref[r, :, own] = pair_grad[:, vc : vc + HEAD_DIM]
    prompt_sum = back_kv[0, 1].astype(jnp.float32)
    for rank in range(1, n):
        prompt_sum = prompt_sum + back_kv[rank, 1].astype(jnp.float32)
    for h in range(kv_heads):
        kc, vc = pair_cols(h)
        own = slice(h * HEAD_DIM, (h + 1) * HEAD_DIM)
        dpk_ref[:, own] = prompt_sum[:prompt_rows, kc : kc + HEAD_DIM].astype(jnp.bfloat16)
        dpv_ref[:, own] = prompt_sum[:prompt_rows, vc : vc + HEAD_DIM].astype(jnp.bfloat16)

    wait_bytes(send_kv.at[0 : n - 1], sem_send.at[0])
    wait_bytes(send_qg.at[0 : n - 1], sem_send.at[1])
    wait_bytes(back_q.at[0 : n - 1], sem_send.at[2])
    wait_bytes(back_kv.at[0 : n - 1], sem_send.at[3])


def kernel_body(*arrays):
    query, key, _, _, prompt_key, _, _, _, _ = arrays
    n = lax.axis_size("seq")
    rows, width = query.shape[1:]
    kv_width = key.shape[2]
    prompt_rows = prompt_key.shape[0]
    slot = -(-prompt_rows // ROW_TILE) * ROW_TILE
    group = width // kv_width
    pieces = (kv_width // HEAD_DIM) * (2 if group % 2 == 0 else 1)
    total = n * rows
    bf16 = jnp.bfloat16
    vmem = pl.BlockSpec(memory_space=pltpu.VMEM)
    smem = pl.BlockSpec(memory_space=pltpu.SMEM)
    return pl.pallas_call(
        functools.partial(kernel, n, pieces, prompt_rows),
        out_shape=(
            jax.ShapeDtypeStruct((1, total, width), bf16),
            jax.ShapeDtypeStruct(query.shape, bf16),
            jax.ShapeDtypeStruct(key.shape, bf16),
            jax.ShapeDtypeStruct(key.shape, bf16),
            jax.ShapeDtypeStruct(prompt_key.shape, bf16),
            jax.ShapeDtypeStruct(prompt_key.shape, bf16),
        ),
        in_specs=[vmem] * 6 + [smem] * 3,
        out_specs=(vmem,) * 6,
        scratch_shapes=[
            pltpu.VMEM((n, 2, rows, width), bf16),
            pltpu.VMEM((n, 2, rows, 2 * kv_width), bf16),
            pltpu.VMEM((2, total, width), bf16),
            pltpu.VMEM((2, total, 2 * kv_width), bf16),
            pltpu.VMEM((total, width), bf16),
            pltpu.VMEM((2, total, 2 * kv_width), bf16),
            pltpu.VMEM((n, rows, width), bf16),
            pltpu.VMEM((n, 2, rows, 2 * kv_width), bf16),
            pltpu.VMEM((2, total + n * slot, HEAD_DIM), jnp.float32),
            pltpu.SemaphoreType.DMA((4,)),
            pltpu.SemaphoreType.DMA,
            pltpu.SemaphoreType.DMA((pieces,)),
            pltpu.SemaphoreType.DMA((2,)),
        ],
        compiler_params=pltpu.CompilerParams(
            collective_id=0, has_side_effects=True, vmem_limit_bytes=40 * 1024 * 1024
        ),
    )(*arrays)


def body(*arrays):
    rows = arrays[0].shape[1]
    slot = -(-arrays[4].shape[0] // ROW_TILE) * ROW_TILE
    if rows % ROW_TILE == 0 and slot == rows:
        return kernel_body(*arrays)
    return collective_body(*arrays)


def solution(mesh):
    placed = (
        P("group", "seq", "head"),
        P("group", "seq", "head"),
        P("group", "seq", "head"),
        P("group", "seq", "head"),
        P(("group", "seq"), "head"),
        P(("group", "seq"), "head"),
        P("group"),
        P("group"),
        P("group"),
    )
    return jax.shard_map(
        body,
        mesh=mesh,
        in_specs=placed,
        out_specs=(
            P(("group", "seq"), None, "head"),
            P("group", "seq", "head"),
            P("group", "seq", "head"),
            P("group", "seq", "head"),
            P(("group", "seq"), "head"),
            P(("group", "seq"), "head"),
        ),
        check_vma=False,
    )
```

```python
import functools

import jax
import jax.numpy as jnp
from jax import lax
from jax.experimental import pallas as pl
from jax.experimental.pallas import tpu as pltpu
from jax.sharding import PartitionSpec as P

HEAD_DIM = 128


NEG_FILL = -1e30


def head_logits(queries, all_keys, allowed, head_index, group_size, scale_factor):
    row_count = queries.shape[0]
    low = head_index * group_size * HEAD_DIM
    high = (head_index + 1) * group_size * HEAD_DIM
    query_head = queries[:, low:high].reshape(row_count, group_size, HEAD_DIM)
    key_head = all_keys[:, head_index * HEAD_DIM : (head_index + 1) * HEAD_DIM]
    logits = (
        jnp.einsum("rhd,kd->rhk", query_head, key_head, preferred_element_type=jnp.float32)
        * scale_factor
    )
    return (query_head, key_head, jnp.where(allowed[:, None, :], logits, NEG_FILL))


def forward(queries, all_keys, all_values, allowed, live_rows, scale_factor):
    row_count = queries.shape[0]
    kv_count = all_keys.shape[1] // HEAD_DIM
    group_size = queries.shape[1] // all_keys.shape[1]
    outputs = []
    totals = []
    for head_index in range(kv_count):
        query_head, key_head, logits = head_logits(
            queries, all_keys, allowed, head_index, group_size, scale_factor
        )
        value_head = all_values[:, head_index * HEAD_DIM : (head_index + 1) * HEAD_DIM]
        row_max = jnp.max(logits, axis=2, keepdims=True)
        log_total = row_max + jnp.log(jnp.sum(jnp.exp(logits - row_max), axis=2, keepdims=True))
        weights = jnp.exp(logits - log_total).astype(jnp.bfloat16)
        mixed = jnp.einsum("rhk,kd->rhd", weights, value_head, preferred_element_type=jnp.float32)
        output_head = jnp.where(live_rows[:, None, None], mixed, 0.0).astype(jnp.bfloat16)
        outputs.append(output_head.reshape(row_count, group_size * HEAD_DIM))
        totals.append(log_total)
    return (jnp.concatenate(outputs, axis=1), totals)


def head_terms(grad_rows, live_rows, output, head_index, group_size):
    row_count = grad_rows.shape[0]
    low = head_index * group_size * HEAD_DIM
    high = (head_index + 1) * group_size * HEAD_DIM
    grad_head = jnp.where(live_rows[:, None], grad_rows[:, low:high], jnp.zeros((), jnp.bfloat16))
    grad_head = grad_head.reshape(row_count, group_size, HEAD_DIM)
    output_head = lax.optimization_barrier(output[:, low:high]).reshape(
        row_count, group_size, HEAD_DIM
    )
    row_dot = jnp.sum(
        grad_head.astype(jnp.float32) * output_head.astype(jnp.float32), axis=2, keepdims=True
    )
    return (grad_head, row_dot)


def backward(
    queries, all_keys, all_values, grad_rows, allowed, live_rows, output, totals, scale_factor
):
    row_count = queries.shape[0]
    kv_count = all_keys.shape[1] // HEAD_DIM
    group_size = queries.shape[1] // all_keys.shape[1]
    query_grads = []
    key_grads = []
    value_grads = []
    for head_index in range(kv_count):
        query_head, key_head, logits = head_logits(
            queries, all_keys, allowed, head_index, group_size, scale_factor
        )
        value_head = all_values[:, head_index * HEAD_DIM : (head_index + 1) * HEAD_DIM]
        prob = jnp.exp(logits - totals[head_index])
        weights = prob.astype(jnp.bfloat16)
        grad_head, row_dot = head_terms(grad_rows, live_rows, output, head_index, group_size)
        spread = jnp.einsum(
            "rhd,kd->rhk", grad_head, value_head, preferred_element_type=jnp.float32
        )
        dlogit = (prob * (spread - row_dot)).astype(jnp.bfloat16)
        query_part = (
            jnp.einsum("rhk,kd->rhd", dlogit, key_head, preferred_element_type=jnp.float32)
            * scale_factor
        )
        query_grads.append(query_part.reshape(row_count, group_size * HEAD_DIM))
        key_grads.append(
            jnp.einsum("rhk,rhd->kd", dlogit, query_head, preferred_element_type=jnp.float32)
            * scale_factor
        )
        value_grads.append(
            jnp.einsum("rhk,rhd->kd", weights, grad_head, preferred_element_type=jnp.float32)
        )
    return (
        jnp.concatenate(query_grads, axis=1),
        jnp.concatenate(key_grads, axis=1),
        jnp.concatenate(value_grads, axis=1),
    )


def collective_body(
    response_query,
    response_key,
    response_value,
    response_grad,
    prompt_key,
    prompt_value,
    lengths,
    home_rank,
    prompt_seen,
):
    rank_count = home_rank.shape[0]
    rank_ids = jnp.arange(rank_count, dtype=jnp.int32)
    resident = jnp.sum(
        jnp.where(home_rank[None, :] == rank_ids[:, None], rank_ids[None, :], 0), axis=1
    )
    own_rank = lax.axis_index("seq")
    scale_factor = 1.0 / HEAD_DIM**0.5
    arrived = (
        lax.all_to_all(response_query[resident], "seq", split_axis=0, concat_axis=1, tiled=True),
        lax.all_to_all(response_key[resident], "seq", split_axis=0, concat_axis=1, tiled=True),
        lax.all_to_all(response_value[resident], "seq", split_axis=0, concat_axis=1, tiled=True),
        lax.all_to_all(response_grad[resident], "seq", split_axis=0, concat_axis=1, tiled=True),
    )
    queries = arrived[0][0]
    own_keys = arrived[1][0]
    own_values = arrived[2][0]
    grad_rows = arrived[3][0]
    own_response = resident[own_rank]
    length = lengths[own_response]
    visible = prompt_seen[own_response]
    max_length = queries.shape[0]
    prompt_rows = prompt_key.shape[0]
    prompt_total = prompt_rows * lax.axis_size("seq")
    positions = jnp.arange(max_length, dtype=jnp.int32)
    prompt_cols = jnp.arange(prompt_total, dtype=jnp.int32)
    seen_part = jnp.broadcast_to(prompt_cols[None, :] < visible, (max_length, prompt_total))
    allowed = jnp.concatenate([seen_part, positions[None, :] <= positions[:, None]], axis=1)
    live_rows = positions < length
    gathered_keys, gathered_values = (
        lax.all_gather(prompt_key, "seq", axis=0, tiled=True),
        lax.all_gather(prompt_value, "seq", axis=0, tiled=True),
    )
    all_keys = jnp.concatenate([gathered_keys, own_keys], axis=0)
    all_values = jnp.concatenate([gathered_values, own_values], axis=0)
    response_out, response_totals = forward(
        queries, all_keys, all_values, allowed, live_rows, scale_factor
    )
    query_grad, key_grad, value_grad = backward(
        queries,
        all_keys,
        all_values,
        grad_rows,
        allowed,
        live_rows,
        response_out,
        response_totals,
        scale_factor,
    )
    key_summed, value_summed = (
        lax.psum_scatter(key_grad[:prompt_total], "seq", scatter_dimension=0, tiled=True),
        lax.psum_scatter(value_grad[:prompt_total], "seq", scatter_dimension=0, tiled=True),
    )
    returned = (
        lax.all_to_all(
            query_grad.astype(jnp.bfloat16)[None], "seq", split_axis=1, concat_axis=0, tiled=True
        ),
        lax.all_to_all(
            key_grad[prompt_total:].astype(jnp.bfloat16)[None],
            "seq",
            split_axis=1,
            concat_axis=0,
            tiled=True,
        ),
        lax.all_to_all(
            value_grad[prompt_total:].astype(jnp.bfloat16)[None],
            "seq",
            split_axis=1,
            concat_axis=0,
            tiled=True,
        ),
    )
    return (
        response_out[None],
        returned[0][home_rank],
        returned[1][home_rank],
        returned[2][home_rank],
        key_summed.astype(jnp.bfloat16),
        value_summed.astype(jnp.bfloat16),
    )


ROW_TILE = 16
MESH = pl.DeviceIdType.MESH


def dot_last(left, right):
    return lax.dot_general(left, right, (((1,), (1,)), ((), ())), preferred_element_type=jnp.float32)


def dot_first(left, right):
    return lax.dot_general(left, right, (((0,), (0,)), ((), ())), preferred_element_type=jnp.float32)


def dot_plain(left, right):
    return lax.dot_general(left, right, (((1,), (0,)), ((), ())), preferred_element_type=jnp.float32)


def wait_bytes(ref, sem):
    pltpu.make_async_copy(ref, ref, sem).wait()


def kernel(
    n, inner, prompt_rows,
    q_hbm, k_hbm, v_hbm, g_hbm, pk_ref, pv_ref, len_hbm, home_hbm, seen_hbm,
    out_ref, back_q, dk_ref, dv_ref, dpk_ref, dpv_ref,
    q_ref, k_ref, v_ref, g_ref, len_ref, home_ref, seen_ref,
    send_qg, send_kv, send_p, in_qg, in_kv, in_p,
    out_send, grad_q, grad_kv, grad_p, back_kv, back_p, acc,
    sem_load, sem_local, sem_send, sem_kv_out, sem_grad_out,
    sem_p, sem_qg, sem_kv, sem_out, sem_q, sem_grad, sem_gp,
):
    me = lax.axis_index("seq")
    outer = n // inner
    mz, mx = lax.div(me, inner), lax.rem(me, inner)
    rows, width = q_ref.shape[1:]
    kv_width = k_ref.shape[2]
    kv_heads = kv_width // HEAD_DIM
    group = width // kv_width
    total = n * rows
    block = inner * rows
    stacked = group * block
    slot = in_p.shape[0] // n
    scale = 1.0 / HEAD_DIM**0.5

    loads = [
        pltpu.make_async_copy(src, dst, sem_load.at[i])
        for i, (src, dst) in enumerate((
            (len_hbm, len_ref), (home_hbm, home_ref), (seen_hbm, seen_ref),
            (k_hbm, k_ref), (v_hbm, v_ref), (q_hbm, q_ref), (g_hbm, g_ref),
        ))
    ]
    for load in loads:
        load.start()
    in_kv[...] = jnp.zeros_like(in_kv)
    back_kv[...] = jnp.zeros_like(back_kv)
    barrier = pltpu.get_barrier_semaphore()
    for step in range(1, n):
        pl.semaphore_signal(
            barrier, inc=1, device_id={"seq": lax.rem(me + step, n)}, device_id_type=MESH
        )

    def send(src, dst, send_sem, recv_sem, peer):
        pltpu.make_async_remote_copy(
            src_ref=src, dst_ref=dst, send_sem=send_sem, recv_sem=recv_sem,
            device_id={"seq": peer}, device_id_type=MESH,
        ).start()

    def tile(index, size):
        return pl.ds(pl.multiple_of(index * size, size), size)

    def pair_cols(head):
        return head * 2 * HEAD_DIM, head * 2 * HEAD_DIM + HEAD_DIM

    prompt_pad = jnp.zeros((slot - prompt_rows, HEAD_DIM), jnp.float32)
    for h in range(kv_heads):
        kc, vc = pair_cols(h)
        own = slice(h * HEAD_DIM, (h + 1) * HEAD_DIM)
        for ref, col in ((pk_ref, kc), (pv_ref, vc)):
            part = ref[:, own].astype(jnp.float32)
            if slot > prompt_rows:
                part = jnp.concatenate([part, prompt_pad], axis=0)
            send_p[:, col : col + HEAD_DIM] = part.astype(jnp.bfloat16)
    for load in loads[:5]:
        load.wait()

    def resident(rank):
        found = jnp.int32(0)
        for r in range(n):
            found = jnp.where(home_ref[r] == rank, jnp.int32(r), found)
        return found

    sources = [resident(rank) for rank in range(n)]
    for rank in range(n):
        key_rows = k_ref[sources[rank]]
        value_rows = v_ref[sources[rank]]
        for h in range(kv_heads):
            kc, vc = pair_cols(h)
            own = slice(h * HEAD_DIM, (h + 1) * HEAD_DIM)
            send_kv[rank, :, kc : kc + HEAD_DIM] = key_rows[:, own]
            send_kv[rank, :, vc : vc + HEAD_DIM] = value_rows[:, own]
    pl.semaphore_wait(barrier, n - 1)

    partner = mz * inner + (inner - 1 - mx)
    own_rows = tile(me, rows)

    def send_keys(stage):
        for step in range(outer):
            @pl.when(mz + step < outer)
            def _():
                for dx in range(inner):
                    home = stage * inner + dx
                    peer = (mz + step) * inner + dx

                    def go():
                        send(send_kv.at[home], in_kv.at[stage, own_rows, :],
                             sem_kv_out.at[step], sem_kv.at[stage, mz], peer)

                    if step == 0:
                        pl.when(mx != dx)(go)
                    else:
                        go()

    send_keys(0)
    for step in range(1, n):
        send(send_p, in_p.at[tile(me, slot), :], sem_send.at[0], sem_p, lax.rem(me + step, n))
    loads[5].wait()
    loads[6].wait()
    for stage in range(outer):
        for dx in range(inner):
            rank = stage * inner + dx
            send_qg[rank, 0] = q_ref[sources[rank]]
            send_qg[rank, 1] = g_ref[sources[rank]]
        send(send_qg.at[stage * inner + inner - 1 - mx], in_qg.at[stage, :, tile(mx, rows), :],
             sem_send.at[1], sem_qg.at[stage], partner)
        if stage > 0:
            send_keys(stage)
        in_qg[stage, :, tile(mx, rows), :] = send_qg[stage * inner + mx]
        in_kv[stage, own_rows, :] = send_kv[stage * inner + mx]
    in_p[tile(me, slot), :] = send_p[...]

    keys_total = total + n * slot
    row_id = lax.broadcasted_iota(jnp.int32, (stacked, keys_total), 0)
    position = mz * block + row_id - (row_id // block) * block
    col_id = lax.broadcasted_iota(jnp.int32, (stacked, keys_total), 1)
    in_prompt = col_id - total
    prompt_slot = in_prompt // slot
    prompt_row = in_prompt - prompt_slot * slot
    prompt_id = prompt_slot * prompt_rows + prompt_row
    far = jnp.int32(2**30)
    prompt_rank = jnp.where(prompt_row < prompt_rows, prompt_id, far)
    ahead = col_id - position
    live_row = lax.broadcasted_iota(jnp.int32, (stacked, HEAD_DIM), 0)
    live_position = mz * block + live_row - (live_row // block) * block

    wait_bytes(in_p.at[0 : (n - 1) * slot, :], sem_p)
    acc[...] = jnp.zeros_like(acc)
    for stage in range(outer):
        home = stage * inner + mx
        source = resident(home)
        length = len_ref[source]
        visible = seen_ref[source]
        allowed = jnp.where(col_id < total, ahead, prompt_rank - visible + 1) <= 0
        live = live_position < length
        for step in range(outer):
            @pl.when(step < mz)
            def _():
                wait_bytes(in_kv.at[stage, 0:block, :], sem_kv.at[stage, step])

            @pl.when(step == mz)
            def _():
                wait_bytes(in_kv.at[stage, 0:rows, :], sem_kv.at[stage, step])
        wait_bytes(in_qg.at[stage, :, 0:rows, :], sem_qg.at[stage])
        for h in range(kv_heads):
            kc, vc = pair_cols(h)
            keys = jnp.concatenate(
                [in_kv[stage, :, kc : kc + HEAD_DIM], in_p[:, kc : kc + HEAD_DIM]], axis=0
            )
            values = jnp.concatenate(
                [in_kv[stage, :, vc : vc + HEAD_DIM], in_p[:, vc : vc + HEAD_DIM]], axis=0
            )
            heads = [
                slice((h * group + a) * HEAD_DIM, (h * group + a + 1) * HEAD_DIM)
                for a in range(group)
            ]
            query = jnp.concatenate([in_qg[stage, 0, :, c] for c in heads], axis=0)
            grad = jnp.concatenate([in_qg[stage, 1, :, c] for c in heads], axis=0)
            grad_wide = jnp.where(live, grad.astype(jnp.float32), 0.0)
            grad = grad_wide.astype(jnp.bfloat16)
            logits = jnp.where(allowed, dot_last(query, keys) * scale, NEG_FILL)
            exped = jnp.exp(logits - jnp.max(logits, axis=1, keepdims=True))
            prob = exped * (1.0 / jnp.sum(exped, axis=1, keepdims=True))
            weights = prob.astype(jnp.bfloat16)
            output = jnp.where(live, dot_plain(weights, values), 0.0).astype(jnp.bfloat16)
            row_dot = jnp.sum(grad_wide * output.astype(jnp.float32), axis=1, keepdims=True)
            dlogit = (prob * (dot_last(grad, values) - row_dot)).astype(jnp.bfloat16)
            dquery = (dot_plain(dlogit, keys) * scale).astype(jnp.bfloat16)
            for a in range(group):
                part = slice(a * block, (a + 1) * block)
                out_send[stage, :, heads[a]] = output[part]
                grad_q[stage, :, heads[a]] = dquery[part]
            dkey = dot_first(dlogit, query) * scale
            dvalue = dot_first(weights, grad)
            for col, part in ((kc, dkey), (vc, dvalue)):
                grad_kv[stage, :, col : col + HEAD_DIM] = part[:total].astype(jnp.bfloat16)
                acc[:, col : col + HEAD_DIM] += part[total:]

        @pl.when(mz != stage)
        def _():
            send(out_send.at[stage], out_ref.at[0, tile(mz, block), :],
                 sem_send.at[2], sem_out, home)

        @pl.when(mz == stage)
        def _():
            pltpu.make_async_copy(
                out_send.at[stage], out_ref.at[0, tile(mz, block), :], sem_local.at[0]
            ).start()

        for step in range(outer):
            @pl.when(mz - step >= 0)
            def _():
                for dx in range(inner):
                    chunk = (mz - step) * inner + dx

                    def go():
                        send(grad_kv.at[stage, tile(chunk, rows), :], back_kv.at[mz, home],
                             sem_grad_out.at[step], sem_grad.at[mz], chunk)

                    if step == 0:
                        pl.when(mx != dx)(go)
                    else:
                        go()
        send(grad_q.at[stage, tile(inner - 1 - mx, rows), :], back_q.at[home],
             sem_send.at[3], sem_q, partner)
        pltpu.make_async_copy(
            grad_q.at[stage, tile(mx, rows), :], back_q.at[home], sem_local.at[1]
        ).start()
        back_kv[mz, home] = grad_kv[stage, own_rows, :]
    grad_p[...] = acc[...].astype(jnp.bfloat16)
    for step in range(1, n):
        peer = lax.rem(me + step, n)
        send(grad_p.at[tile(peer, slot), :], back_p.at[me], sem_send.at[4], sem_gp, peer)
    back_p[me] = grad_p[tile(me, slot), :]

    for step in range(outer):
        @pl.when(step > mz)
        def _():
            wait_bytes(back_kv.at[step], sem_grad.at[step])

        @pl.when(step == mz)
        def _():
            wait_bytes(back_kv.at[step, 0:outer], sem_grad.at[step])
    for r in range(n):
        home = home_ref[r]
        summed = back_kv[0, home].astype(jnp.float32)
        for step in range(1, outer):
            summed = summed + back_kv[step, home].astype(jnp.float32)
        summed = summed.astype(jnp.bfloat16)
        for h in range(kv_heads):
            kc, vc = pair_cols(h)
            own = slice(h * HEAD_DIM, (h + 1) * HEAD_DIM)
            dk_ref[r, :, own] = summed[:, kc : kc + HEAD_DIM]
            dv_ref[r, :, own] = summed[:, vc : vc + HEAD_DIM]
    wait_bytes(back_p.at[0 : n - 1], sem_gp)
    prompt_sum = back_p[0].astype(jnp.float32)
    for rank in range(1, n):
        prompt_sum = prompt_sum + back_p[rank].astype(jnp.float32)
    for h in range(kv_heads):
        kc, vc = pair_cols(h)
        own = slice(h * HEAD_DIM, (h + 1) * HEAD_DIM)
        dpk_ref[:, own] = prompt_sum[:prompt_rows, kc : kc + HEAD_DIM].astype(jnp.bfloat16)
        dpv_ref[:, own] = prompt_sum[:prompt_rows, vc : vc + HEAD_DIM].astype(jnp.bfloat16)

    wait_bytes(out_send.at[0], sem_local.at[0])
    wait_bytes(back_q.at[0:outer], sem_local.at[1])
    wait_bytes(out_send.at[0 : outer - 1], sem_out)
    wait_bytes(back_q.at[0:outer], sem_q)
    wait_bytes(back_p.at[0 : n - 1], sem_send.at[0])
    wait_bytes(in_qg.at[:, :, 0:rows, :], sem_send.at[1])
    wait_bytes(out_send.at[0 : outer - 1], sem_send.at[2])
    wait_bytes(back_q.at[0:outer], sem_send.at[3])
    wait_bytes(back_p.at[0 : n - 1], sem_send.at[4])
    for sem in (sem_kv_out, sem_grad_out):
        for step in range(outer):
            reached = mz + step < outer if sem is sem_kv_out else mz - step >= 0

            @pl.when(reached)
            def _():
                wait_bytes(send_kv.at[0 : outer if step == 0 else n], sem.at[step])


def place_kernel(
    n, out_in, back_q, dk_in, dv_in, dpk_in, dpv_in, home_hbm,
    out_ref, dq_ref, dk_ref, dv_ref, dpk_ref, dpv_ref, home_ref, sems, sem_row, sem_home,
):
    ranks = pltpu.make_async_copy(home_hbm, home_ref, sem_home)
    ranks.start()
    pairs = ((out_in, out_ref), (dk_in, dk_ref), (dv_in, dv_ref), (dpk_in, dpk_ref), (dpv_in, dpv_ref))
    copies = [pltpu.make_async_copy(src, dst, sems.at[i]) for i, (src, dst) in enumerate(pairs)]
    for copy in copies:
        copy.start()
    ranks.wait()
    moves = [
        pltpu.make_async_copy(back_q.at[home_ref[r]], dq_ref.at[r], sem_row.at[r]) for r in range(n)
    ]
    for copy in moves:
        copy.start()
    for copy in copies + moves:
        copy.wait()


def kernel_body(*arrays):
    query, key, _, _, prompt_key, _, lengths, home_rank, _ = arrays
    n = lax.axis_size("seq")
    inner = 2
    outer = n // inner
    rows, width = query.shape[1:]
    kv_width = key.shape[2]
    prompt_rows = prompt_key.shape[0]
    slot = -(-prompt_rows // ROW_TILE) * ROW_TILE
    total = n * rows
    bf16 = jnp.bfloat16
    vmem = pl.BlockSpec(memory_space=pltpu.VMEM)
    hbm = pl.BlockSpec(memory_space=pltpu.HBM)
    shapes = (
        jax.ShapeDtypeStruct((1, total, width), bf16),
        jax.ShapeDtypeStruct(query.shape, bf16),
        jax.ShapeDtypeStruct(key.shape, bf16),
        jax.ShapeDtypeStruct(key.shape, bf16),
        jax.ShapeDtypeStruct(prompt_key.shape, bf16),
        jax.ShapeDtypeStruct(prompt_key.shape, bf16),
    )
    dma = pltpu.SemaphoreType.DMA
    results = pl.pallas_call(
        functools.partial(kernel, n, inner, prompt_rows),
        out_shape=shapes,
        in_specs=[hbm] * 4 + [vmem] * 2 + [hbm] * 3,
        out_specs=(hbm,) * 2 + (vmem,) * 4,
        scratch_shapes=[
            pltpu.VMEM(query.shape, bf16),
            pltpu.VMEM(key.shape, bf16),
            pltpu.VMEM(key.shape, bf16),
            pltpu.VMEM(query.shape, bf16),
            pltpu.SMEM(lengths.shape, jnp.int32),
            pltpu.SMEM(lengths.shape, jnp.int32),
            pltpu.SMEM(lengths.shape, jnp.int32),
            pltpu.VMEM((n, 2, rows, width), bf16),
            pltpu.VMEM((n, rows, 2 * kv_width), bf16),
            pltpu.VMEM((slot, 2 * kv_width), bf16),
            pltpu.VMEM((outer, 2, inner * rows, width), bf16),
            pltpu.VMEM((outer, total, 2 * kv_width), bf16),
            pltpu.VMEM((n * slot, 2 * kv_width), bf16),
            pltpu.VMEM((outer, inner * rows, width), bf16),
            pltpu.VMEM((outer, inner * rows, width), bf16),
            pltpu.VMEM((outer, total, 2 * kv_width), bf16),
            pltpu.VMEM((n * slot, 2 * kv_width), bf16),
            pltpu.VMEM((outer, n, rows, 2 * kv_width), bf16),
            pltpu.VMEM((n, slot, 2 * kv_width), bf16),
            pltpu.VMEM((n * slot, 2 * kv_width), jnp.float32),
            dma((7,)), dma((2,)), dma((5,)), dma((outer,)), dma((outer,)),
            dma, dma((outer,)), dma((outer, outer)), dma, dma, dma((outer,)), dma,
        ],
        compiler_params=pltpu.CompilerParams(
            collective_id=0, has_side_effects=True, vmem_limit_bytes=48 * 1024 * 1024
        ),
    )(*arrays)
    return pl.pallas_call(
        functools.partial(place_kernel, n),
        out_shape=shapes,
        in_specs=[hbm] * 7,
        out_specs=(hbm,) * 6,
        scratch_shapes=[pltpu.SMEM(home_rank.shape, jnp.int32), dma((5,)), dma((n,)), dma],
    )(*results, home_rank)


def body(*arrays):
    rows = arrays[0].shape[1]
    slot = -(-arrays[4].shape[0] // ROW_TILE) * ROW_TILE
    if rows % ROW_TILE == 0 and slot == rows and lax.axis_size("seq") % 2 == 0:
        return kernel_body(*arrays)
    return collective_body(*arrays)


def solution(mesh):
    placed = (
        P("group", "seq", "head"),
        P("group", "seq", "head"),
        P("group", "seq", "head"),
        P("group", "seq", "head"),
        P(("group", "seq"), "head"),
        P(("group", "seq"), "head"),
        P("group"),
        P("group"),
        P("group"),
    )
    return jax.shard_map(
        body,
        mesh=mesh,
        in_specs=placed,
        out_specs=(
            P(("group", "seq"), None, "head"),
            P("group", "seq", "head"),
            P("group", "seq", "head"),
            P("group", "seq", "head"),
            P(("group", "seq"), "head"),
            P(("group", "seq"), "head"),
        ),
        check_vma=False,
    )
```

```python
import functools

import jax
import jax.numpy as jnp
from jax import lax
from jax.experimental import pallas as pl
from jax.experimental.pallas import tpu as pltpu
from jax.sharding import PartitionSpec as P

HEAD_DIM = 128


NEG_FILL = -1e30


def head_logits(queries, all_keys, allowed, head_index, group_size, scale_factor):
    row_count = queries.shape[0]
    low = head_index * group_size * HEAD_DIM
    high = (head_index + 1) * group_size * HEAD_DIM
    query_head = queries[:, low:high].reshape(row_count, group_size, HEAD_DIM)
    key_head = all_keys[:, head_index * HEAD_DIM : (head_index + 1) * HEAD_DIM]
    logits = (
        jnp.einsum("rhd,kd->rhk", query_head, key_head, preferred_element_type=jnp.float32)
        * scale_factor
    )
    return (query_head, key_head, jnp.where(allowed[:, None, :], logits, NEG_FILL))


def forward(queries, all_keys, all_values, allowed, live_rows, scale_factor):
    row_count = queries.shape[0]
    kv_count = all_keys.shape[1] // HEAD_DIM
    group_size = queries.shape[1] // all_keys.shape[1]
    outputs = []
    totals = []
    for head_index in range(kv_count):
        query_head, key_head, logits = head_logits(
            queries, all_keys, allowed, head_index, group_size, scale_factor
        )
        value_head = all_values[:, head_index * HEAD_DIM : (head_index + 1) * HEAD_DIM]
        row_max = jnp.max(logits, axis=2, keepdims=True)
        log_total = row_max + jnp.log(jnp.sum(jnp.exp(logits - row_max), axis=2, keepdims=True))
        weights = jnp.exp(logits - log_total).astype(jnp.bfloat16)
        mixed = jnp.einsum("rhk,kd->rhd", weights, value_head, preferred_element_type=jnp.float32)
        output_head = jnp.where(live_rows[:, None, None], mixed, 0.0).astype(jnp.bfloat16)
        outputs.append(output_head.reshape(row_count, group_size * HEAD_DIM))
        totals.append(log_total)
    return (jnp.concatenate(outputs, axis=1), totals)


def head_terms(grad_rows, live_rows, output, head_index, group_size):
    row_count = grad_rows.shape[0]
    low = head_index * group_size * HEAD_DIM
    high = (head_index + 1) * group_size * HEAD_DIM
    grad_head = jnp.where(live_rows[:, None], grad_rows[:, low:high], jnp.zeros((), jnp.bfloat16))
    grad_head = grad_head.reshape(row_count, group_size, HEAD_DIM)
    output_head = lax.optimization_barrier(output[:, low:high]).reshape(
        row_count, group_size, HEAD_DIM
    )
    row_dot = jnp.sum(
        grad_head.astype(jnp.float32) * output_head.astype(jnp.float32), axis=2, keepdims=True
    )
    return (grad_head, row_dot)


def backward(
    queries, all_keys, all_values, grad_rows, allowed, live_rows, output, totals, scale_factor
):
    row_count = queries.shape[0]
    kv_count = all_keys.shape[1] // HEAD_DIM
    group_size = queries.shape[1] // all_keys.shape[1]
    query_grads = []
    key_grads = []
    value_grads = []
    for head_index in range(kv_count):
        query_head, key_head, logits = head_logits(
            queries, all_keys, allowed, head_index, group_size, scale_factor
        )
        value_head = all_values[:, head_index * HEAD_DIM : (head_index + 1) * HEAD_DIM]
        prob = jnp.exp(logits - totals[head_index])
        weights = prob.astype(jnp.bfloat16)
        grad_head, row_dot = head_terms(grad_rows, live_rows, output, head_index, group_size)
        spread = jnp.einsum(
            "rhd,kd->rhk", grad_head, value_head, preferred_element_type=jnp.float32
        )
        dlogit = (prob * (spread - row_dot)).astype(jnp.bfloat16)
        query_part = (
            jnp.einsum("rhk,kd->rhd", dlogit, key_head, preferred_element_type=jnp.float32)
            * scale_factor
        )
        query_grads.append(query_part.reshape(row_count, group_size * HEAD_DIM))
        key_grads.append(
            jnp.einsum("rhk,rhd->kd", dlogit, query_head, preferred_element_type=jnp.float32)
            * scale_factor
        )
        value_grads.append(
            jnp.einsum("rhk,rhd->kd", weights, grad_head, preferred_element_type=jnp.float32)
        )
    return (
        jnp.concatenate(query_grads, axis=1),
        jnp.concatenate(key_grads, axis=1),
        jnp.concatenate(value_grads, axis=1),
    )


def collective_body(
    response_query,
    response_key,
    response_value,
    response_grad,
    prompt_key,
    prompt_value,
    lengths,
    home_rank,
    prompt_seen,
):
    rank_count = home_rank.shape[0]
    rank_ids = jnp.arange(rank_count, dtype=jnp.int32)
    resident = jnp.sum(
        jnp.where(home_rank[None, :] == rank_ids[:, None], rank_ids[None, :], 0), axis=1
    )
    own_rank = lax.axis_index("seq")
    scale_factor = 1.0 / HEAD_DIM**0.5
    arrived = (
        lax.all_to_all(response_query[resident], "seq", split_axis=0, concat_axis=1, tiled=True),
        lax.all_to_all(response_key[resident], "seq", split_axis=0, concat_axis=1, tiled=True),
        lax.all_to_all(response_value[resident], "seq", split_axis=0, concat_axis=1, tiled=True),
        lax.all_to_all(response_grad[resident], "seq", split_axis=0, concat_axis=1, tiled=True),
    )
    queries = arrived[0][0]
    own_keys = arrived[1][0]
    own_values = arrived[2][0]
    grad_rows = arrived[3][0]
    own_response = resident[own_rank]
    length = lengths[own_response]
    visible = prompt_seen[own_response]
    max_length = queries.shape[0]
    prompt_rows = prompt_key.shape[0]
    prompt_total = prompt_rows * lax.axis_size("seq")
    positions = jnp.arange(max_length, dtype=jnp.int32)
    prompt_cols = jnp.arange(prompt_total, dtype=jnp.int32)
    seen_part = jnp.broadcast_to(prompt_cols[None, :] < visible, (max_length, prompt_total))
    allowed = jnp.concatenate([seen_part, positions[None, :] <= positions[:, None]], axis=1)
    live_rows = positions < length
    gathered_keys, gathered_values = (
        lax.all_gather(prompt_key, "seq", axis=0, tiled=True),
        lax.all_gather(prompt_value, "seq", axis=0, tiled=True),
    )
    all_keys = jnp.concatenate([gathered_keys, own_keys], axis=0)
    all_values = jnp.concatenate([gathered_values, own_values], axis=0)
    response_out, response_totals = forward(
        queries, all_keys, all_values, allowed, live_rows, scale_factor
    )
    query_grad, key_grad, value_grad = backward(
        queries,
        all_keys,
        all_values,
        grad_rows,
        allowed,
        live_rows,
        response_out,
        response_totals,
        scale_factor,
    )
    key_summed, value_summed = (
        lax.psum_scatter(key_grad[:prompt_total], "seq", scatter_dimension=0, tiled=True),
        lax.psum_scatter(value_grad[:prompt_total], "seq", scatter_dimension=0, tiled=True),
    )
    returned = (
        lax.all_to_all(
            query_grad.astype(jnp.bfloat16)[None], "seq", split_axis=1, concat_axis=0, tiled=True
        ),
        lax.all_to_all(
            key_grad[prompt_total:].astype(jnp.bfloat16)[None],
            "seq",
            split_axis=1,
            concat_axis=0,
            tiled=True,
        ),
        lax.all_to_all(
            value_grad[prompt_total:].astype(jnp.bfloat16)[None],
            "seq",
            split_axis=1,
            concat_axis=0,
            tiled=True,
        ),
    )
    return (
        response_out[None],
        returned[0][home_rank],
        returned[1][home_rank],
        returned[2][home_rank],
        key_summed.astype(jnp.bfloat16),
        value_summed.astype(jnp.bfloat16),
    )


ROW_TILE = 16
VMEM_BYTES = 64 * 1024 * 1024 - 256 * 1024
MESH = pl.DeviceIdType.MESH


def dot_last(left, right):
    return lax.dot_general(left, right, (((1,), (1,)), ((), ())), preferred_element_type=jnp.float32)


def dot_first(left, right):
    return lax.dot_general(left, right, (((0,), (0,)), ((), ())), preferred_element_type=jnp.float32)


def dot_plain(left, right):
    return lax.dot_general(left, right, (((1,), (0,)), ((), ())), preferred_element_type=jnp.float32)


def wait_bytes(ref, sem):
    pltpu.make_async_copy(ref, ref, sem).wait()


def kernel(
    n, inner, prompt_rows,
    q_hbm, k_hbm, v_hbm, g_hbm, pk_hbm, pv_hbm, len_hbm, home_hbm, seen_hbm,
    out_ref, back_q, dk_hbm, dv_hbm, dpk_hbm, dpv_hbm,
    q_ref, k_ref, v_ref, g_ref, len_ref, home_ref, seen_ref,
    pk_ref, pv_ref, dk_ref, dv_ref, dpk_ref, dpv_ref,
    send_qg, send_kv, send_p, in_qg, in_kv, in_p,
    out_send, grad_q, grad_kv, grad_p, back_kv, back_p, acc,
    sem_load, sem_local, sem_send, sem_kv_out, sem_grad_out,
    sem_p, sem_qg, sem_kv, sem_out, sem_q, sem_grad, sem_gp,
):
    me = lax.axis_index("seq")
    outer = n // inner
    mz, mx = lax.div(me, inner), lax.rem(me, inner)
    rows, width = q_ref.shape[1:]
    kv_width = k_ref.shape[2]
    kv_heads = kv_width // HEAD_DIM
    group = width // kv_width
    total = n * rows
    block = inner * rows
    stacked = group * block
    slot = in_p.shape[0] // n
    scale = 1.0 / HEAD_DIM**0.5

    loads = [
        pltpu.make_async_copy(src, dst, sem_load.at[i])
        for i, (src, dst) in enumerate((
            (len_hbm, len_ref), (home_hbm, home_ref), (seen_hbm, seen_ref),
            (k_hbm, k_ref), (v_hbm, v_ref), (pk_hbm, pk_ref), (pv_hbm, pv_ref),
            (q_hbm, q_ref), (g_hbm, g_ref),
        ))
    ]
    for load in loads:
        load.start()
    in_kv[...] = jnp.zeros_like(in_kv)
    back_kv[...] = jnp.zeros_like(back_kv)
    barrier = pltpu.get_barrier_semaphore()
    for step in range(1, n):
        pl.semaphore_signal(
            barrier, inc=1, device_id={"seq": lax.rem(me + step, n)}, device_id_type=MESH
        )

    def send(src, dst, send_sem, recv_sem, peer):
        pltpu.make_async_remote_copy(
            src_ref=src, dst_ref=dst, send_sem=send_sem, recv_sem=recv_sem,
            device_id={"seq": peer}, device_id_type=MESH,
        ).start()

    def tile(index, size):
        return pl.ds(pl.multiple_of(index * size, size), size)

    def pair_cols(head):
        return head * 2 * HEAD_DIM, head * 2 * HEAD_DIM + HEAD_DIM

    for load in loads[:7]:
        load.wait()
    prompt_pad = jnp.zeros((slot - prompt_rows, HEAD_DIM), jnp.float32)
    for h in range(kv_heads):
        kc, vc = pair_cols(h)
        own = slice(h * HEAD_DIM, (h + 1) * HEAD_DIM)
        for ref, col in ((pk_ref, kc), (pv_ref, vc)):
            part = ref[:, own].astype(jnp.float32)
            if slot > prompt_rows:
                part = jnp.concatenate([part, prompt_pad], axis=0)
            send_p[:, col : col + HEAD_DIM] = part.astype(jnp.bfloat16)

    def resident(rank):
        found = jnp.int32(0)
        for r in range(n):
            found = jnp.where(home_ref[r] == rank, jnp.int32(r), found)
        return found

    sources = [resident(rank) for rank in range(n)]
    for rank in range(n):
        key_rows = k_ref[sources[rank]]
        value_rows = v_ref[sources[rank]]
        for h in range(kv_heads):
            kc, vc = pair_cols(h)
            own = slice(h * HEAD_DIM, (h + 1) * HEAD_DIM)
            send_kv[rank, :, kc : kc + HEAD_DIM] = key_rows[:, own]
            send_kv[rank, :, vc : vc + HEAD_DIM] = value_rows[:, own]
    pl.semaphore_wait(barrier, n - 1)

    partner = mz * inner + (inner - 1 - mx)
    own_rows = tile(me, rows)

    def send_keys(stage):
        for step in range(outer):
            @pl.when(mz + step < outer)
            def _():
                for dx in range(inner):
                    home = stage * inner + dx
                    peer = (mz + step) * inner + dx

                    def go():
                        send(send_kv.at[home], in_kv.at[stage, own_rows, :],
                             sem_kv_out.at[step], sem_kv.at[stage, mz], peer)

                    if step == 0:
                        pl.when(mx != dx)(go)
                    else:
                        go()

    send_keys(0)
    for step in range(1, n):
        send(send_p, in_p.at[tile(me, slot), :], sem_send.at[0], sem_p, lax.rem(me + step, n))
    loads[7].wait()
    loads[8].wait()
    for stage in range(outer):
        for dx in range(inner):
            rank = stage * inner + dx
            send_qg[rank, 0] = q_ref[sources[rank]]
            send_qg[rank, 1] = g_ref[sources[rank]]
        send(send_qg.at[stage * inner + inner - 1 - mx], in_qg.at[stage, :, tile(mx, rows), :],
             sem_send.at[1], sem_qg.at[stage], partner)
        if stage > 0:
            send_keys(stage)
        in_qg[stage, :, tile(mx, rows), :] = send_qg[stage * inner + mx]
        in_kv[stage, own_rows, :] = send_kv[stage * inner + mx]
    in_p[tile(me, slot), :] = send_p[...]

    keys_total = total + n * slot
    row_id = lax.broadcasted_iota(jnp.int32, (stacked, keys_total), 0)
    position = mz * block + row_id - (row_id // block) * block
    col_id = lax.broadcasted_iota(jnp.int32, (stacked, keys_total), 1)
    in_prompt = col_id - total
    prompt_slot = in_prompt // slot
    prompt_row = in_prompt - prompt_slot * slot
    prompt_id = prompt_slot * prompt_rows + prompt_row
    far = jnp.int32(2**30)
    prompt_rank = jnp.where(prompt_row < prompt_rows, prompt_id, far)
    ahead = col_id - position
    live_row = lax.broadcasted_iota(jnp.int32, (stacked, HEAD_DIM), 0)
    live_position = mz * block + live_row - (live_row // block) * block

    wait_bytes(in_p.at[0 : (n - 1) * slot, :], sem_p)
    acc[...] = jnp.zeros_like(acc)
    for stage in range(outer):
        home = stage * inner + mx
        source = resident(home)
        length = len_ref[source]
        visible = seen_ref[source]
        allowed = jnp.where(col_id < total, ahead, prompt_rank - visible + 1) <= 0
        live = live_position < length
        for step in range(outer):
            @pl.when(step < mz)
            def _():
                wait_bytes(in_kv.at[stage, 0:block, :], sem_kv.at[stage, step])

            @pl.when(step == mz)
            def _():
                wait_bytes(in_kv.at[stage, 0:rows, :], sem_kv.at[stage, step])
        wait_bytes(in_qg.at[stage, :, 0:rows, :], sem_qg.at[stage])
        for h in range(kv_heads):
            kc, vc = pair_cols(h)
            keys = jnp.concatenate(
                [in_kv[stage, :, kc : kc + HEAD_DIM], in_p[:, kc : kc + HEAD_DIM]], axis=0
            )
            values = jnp.concatenate(
                [in_kv[stage, :, vc : vc + HEAD_DIM], in_p[:, vc : vc + HEAD_DIM]], axis=0
            )
            heads = [
                slice((h * group + a) * HEAD_DIM, (h * group + a + 1) * HEAD_DIM)
                for a in range(group)
            ]
            query = jnp.concatenate([in_qg[stage, 0, :, c] for c in heads], axis=0)
            grad = jnp.concatenate([in_qg[stage, 1, :, c] for c in heads], axis=0)
            grad_wide = jnp.where(live, grad.astype(jnp.float32), 0.0)
            grad = grad_wide.astype(jnp.bfloat16)
            logits = jnp.where(allowed, dot_last(query, keys) * scale, NEG_FILL)
            exped = jnp.exp(logits - jnp.max(logits, axis=1, keepdims=True))
            prob = exped * (1.0 / jnp.sum(exped, axis=1, keepdims=True))
            weights = prob.astype(jnp.bfloat16)
            output = jnp.where(live, dot_plain(weights, values), 0.0).astype(jnp.bfloat16)
            row_dot = jnp.sum(grad_wide * output.astype(jnp.float32), axis=1, keepdims=True)
            dlogit = (prob * (dot_last(grad, values) - row_dot)).astype(jnp.bfloat16)
            dquery = (dot_plain(dlogit, keys) * scale).astype(jnp.bfloat16)
            for a in range(group):
                part = slice(a * block, (a + 1) * block)
                out_send[stage, :, heads[a]] = output[part]
                grad_q[stage, :, heads[a]] = dquery[part]
            dkey = dot_first(dlogit, query) * scale
            dvalue = dot_first(weights, grad)
            for col, part in ((kc, dkey), (vc, dvalue)):
                grad_kv[stage, :, col : col + HEAD_DIM] = part[:total].astype(jnp.bfloat16)
                acc[:, col : col + HEAD_DIM] += part[total:]

        @pl.when(mz != stage)
        def _():
            send(out_send.at[stage], out_ref.at[0, tile(mz, block), :],
                 sem_send.at[2], sem_out, home)

        @pl.when(mz == stage)
        def _():
            pltpu.make_async_copy(
                out_send.at[stage], out_ref.at[0, tile(mz, block), :], sem_local.at[0]
            ).start()

        for step in range(outer):
            @pl.when(mz - step >= 0)
            def _():
                for dx in range(inner):
                    chunk = (mz - step) * inner + dx

                    def go():
                        send(grad_kv.at[stage, tile(chunk, rows), :], back_kv.at[mz, home],
                             sem_grad_out.at[step], sem_grad.at[mz], chunk)

                    if step == 0:
                        pl.when(mx != dx)(go)
                    else:
                        go()
        send(grad_q.at[stage, tile(inner - 1 - mx, rows), :], back_q.at[home],
             sem_send.at[3], sem_q, partner)
        pltpu.make_async_copy(
            grad_q.at[stage, tile(mx, rows), :], back_q.at[home], sem_local.at[1]
        ).start()
        back_kv[mz, home] = grad_kv[stage, own_rows, :]
    grad_p[...] = acc[...].astype(jnp.bfloat16)
    for step in range(1, n):
        peer = lax.rem(me + step, n)
        send(grad_p.at[tile(peer, slot), :], back_p.at[me], sem_send.at[4], sem_gp, peer)
    back_p[me] = grad_p[tile(me, slot), :]

    for step in range(outer):
        @pl.when(step > mz)
        def _():
            wait_bytes(back_kv.at[step], sem_grad.at[step])

        @pl.when(step == mz)
        def _():
            wait_bytes(back_kv.at[step, 0:outer], sem_grad.at[step])
    for r in range(n):
        home = home_ref[r]
        summed = back_kv[0, home].astype(jnp.float32)
        for step in range(1, outer):
            summed = summed + back_kv[step, home].astype(jnp.float32)
        summed = summed.astype(jnp.bfloat16)
        for h in range(kv_heads):
            kc, vc = pair_cols(h)
            own = slice(h * HEAD_DIM, (h + 1) * HEAD_DIM)
            dk_ref[r, :, own] = summed[:, kc : kc + HEAD_DIM]
            dv_ref[r, :, own] = summed[:, vc : vc + HEAD_DIM]
    wait_bytes(back_p.at[0 : n - 1], sem_gp)
    prompt_sum = back_p[0].astype(jnp.float32)
    for rank in range(1, n):
        prompt_sum = prompt_sum + back_p[rank].astype(jnp.float32)
    for h in range(kv_heads):
        kc, vc = pair_cols(h)
        own = slice(h * HEAD_DIM, (h + 1) * HEAD_DIM)
        dpk_ref[:, own] = prompt_sum[:prompt_rows, kc : kc + HEAD_DIM].astype(jnp.bfloat16)
        dpv_ref[:, own] = prompt_sum[:prompt_rows, vc : vc + HEAD_DIM].astype(jnp.bfloat16)

    stores = [
        pltpu.make_async_copy(src, dst, sem_load.at[i])
        for i, (src, dst) in enumerate((
            (dk_ref, dk_hbm), (dv_ref, dv_hbm), (dpk_ref, dpk_hbm), (dpv_ref, dpv_hbm),
        ))
    ]
    for store in stores:
        store.start()
    wait_bytes(out_send.at[0], sem_local.at[0])
    wait_bytes(back_q.at[0:outer], sem_local.at[1])
    wait_bytes(out_send.at[0 : outer - 1], sem_out)
    wait_bytes(back_q.at[0:outer], sem_q)
    wait_bytes(back_p.at[0 : n - 1], sem_send.at[0])
    wait_bytes(in_qg.at[:, :, 0:rows, :], sem_send.at[1])
    wait_bytes(out_send.at[0 : outer - 1], sem_send.at[2])
    wait_bytes(back_q.at[0:outer], sem_send.at[3])
    wait_bytes(back_p.at[0 : n - 1], sem_send.at[4])
    for sem in (sem_kv_out, sem_grad_out):
        for step in range(outer):
            reached = mz + step < outer if sem is sem_kv_out else mz - step >= 0

            @pl.when(reached)
            def _():
                wait_bytes(send_kv.at[0 : outer if step == 0 else n], sem.at[step])
    for store in stores:
        store.wait()


def place_kernel(n, *refs):
    sources, home_hbm = refs[:6], refs[6]
    results, held, home_ref = refs[7:13], refs[13:19], refs[19]
    sem_in, sem_out, sem_row, sem_home = refs[20:]
    ranks = pltpu.make_async_copy(home_hbm, home_ref, sem_home)
    ranks.start()
    reads = [
        pltpu.make_async_copy(src, dst, sem_in.at[i]) for i, (src, dst) in enumerate(zip(sources, held))
    ]
    for copy in reads:
        copy.start()
    writes = []
    for i in (0, 2, 3, 4, 5):
        reads[i].wait()
        writes.append(pltpu.make_async_copy(held[i], results[i], sem_out.at[i]))
        writes[-1].start()
    reads[1].wait()
    ranks.wait()
    for r in range(n):
        writes.append(pltpu.make_async_copy(held[1].at[home_ref[r]], results[1].at[r], sem_row.at[r]))
        writes[-1].start()
    for copy in writes:
        copy.wait()


def kernel_body(*arrays):
    query, key, _, _, prompt_key, _, lengths, home_rank, _ = arrays
    n = lax.axis_size("seq")
    inner = 2
    outer = n // inner
    rows, width = query.shape[1:]
    kv_width = key.shape[2]
    prompt_rows = prompt_key.shape[0]
    slot = -(-prompt_rows // ROW_TILE) * ROW_TILE
    total = n * rows
    bf16 = jnp.bfloat16
    hbm = pl.BlockSpec(memory_space=pltpu.HBM)
    shapes = (
        jax.ShapeDtypeStruct((1, total, width), bf16),
        jax.ShapeDtypeStruct(query.shape, bf16),
        jax.ShapeDtypeStruct(key.shape, bf16),
        jax.ShapeDtypeStruct(key.shape, bf16),
        jax.ShapeDtypeStruct(prompt_key.shape, bf16),
        jax.ShapeDtypeStruct(prompt_key.shape, bf16),
    )
    dma = pltpu.SemaphoreType.DMA
    results = pl.pallas_call(
        functools.partial(kernel, n, inner, prompt_rows),
        out_shape=shapes,
        in_specs=[hbm] * 9,
        out_specs=(hbm,) * 6,
        scratch_shapes=[
            pltpu.VMEM(query.shape, bf16),
            pltpu.VMEM(key.shape, bf16),
            pltpu.VMEM(key.shape, bf16),
            pltpu.VMEM(query.shape, bf16),
            pltpu.SMEM(lengths.shape, jnp.int32),
            pltpu.SMEM(lengths.shape, jnp.int32),
            pltpu.SMEM(lengths.shape, jnp.int32),
            pltpu.VMEM(prompt_key.shape, bf16),
            pltpu.VMEM(prompt_key.shape, bf16),
            *(pltpu.VMEM(shape.shape, bf16) for shape in shapes[2:]),
            pltpu.VMEM((n, 2, rows, width), bf16),
            pltpu.VMEM((n, rows, 2 * kv_width), bf16),
            pltpu.VMEM((slot, 2 * kv_width), bf16),
            pltpu.VMEM((outer, 2, inner * rows, width), bf16),
            pltpu.VMEM((outer, total, 2 * kv_width), bf16),
            pltpu.VMEM((n * slot, 2 * kv_width), bf16),
            pltpu.VMEM((outer, inner * rows, width), bf16),
            pltpu.VMEM((outer, inner * rows, width), bf16),
            pltpu.VMEM((outer, total, 2 * kv_width), bf16),
            pltpu.VMEM((n * slot, 2 * kv_width), bf16),
            pltpu.VMEM((outer, n, rows, 2 * kv_width), bf16),
            pltpu.VMEM((n, slot, 2 * kv_width), bf16),
            pltpu.VMEM((n * slot, 2 * kv_width), jnp.float32),
            dma((9,)), dma((2,)), dma((5,)), dma((outer,)), dma((outer,)),
            dma, dma((outer,)), dma((outer, outer)), dma, dma, dma((outer,)), dma,
        ],
        compiler_params=pltpu.CompilerParams(
            collective_id=0, has_side_effects=True, vmem_limit_bytes=VMEM_BYTES
        ),
    )(*arrays)
    return pl.pallas_call(
        functools.partial(place_kernel, n),
        out_shape=shapes,
        in_specs=[hbm] * 7,
        out_specs=(hbm,) * 6,
        scratch_shapes=[
            *(pltpu.VMEM(shape.shape, bf16) for shape in shapes),
            pltpu.SMEM(home_rank.shape, jnp.int32),
            dma((6,)), dma((6,)), dma((n,)), dma,
        ],
        compiler_params=pltpu.CompilerParams(vmem_limit_bytes=VMEM_BYTES),
    )(*results, home_rank)


def body(*arrays):
    rows = arrays[0].shape[1]
    slot = -(-arrays[4].shape[0] // ROW_TILE) * ROW_TILE
    if rows % ROW_TILE == 0 and slot == rows and lax.axis_size("seq") % 2 == 0:
        return kernel_body(*arrays)
    return collective_body(*arrays)


def solution(mesh):
    placed = (
        P("group", "seq", "head"),
        P("group", "seq", "head"),
        P("group", "seq", "head"),
        P("group", "seq", "head"),
        P(("group", "seq"), "head"),
        P(("group", "seq"), "head"),
        P("group"),
        P("group"),
        P("group"),
    )
    return jax.shard_map(
        body,
        mesh=mesh,
        in_specs=placed,
        out_specs=(
            P(("group", "seq"), None, "head"),
            P("group", "seq", "head"),
            P("group", "seq", "head"),
            P("group", "seq", "head"),
            P(("group", "seq"), "head"),
            P(("group", "seq"), "head"),
        ),
        check_vma=False,
    )
```

```python
import functools

import jax
import jax.numpy as jnp
from jax import lax
from jax.experimental import pallas as pl
from jax.experimental.pallas import tpu as pltpu
from jax.sharding import PartitionSpec as P

HEAD_DIM = 128


NEG_FILL = -1e30


def head_logits(queries, all_keys, allowed, head_index, group_size, scale_factor):
    row_count = queries.shape[0]
    low = head_index * group_size * HEAD_DIM
    high = (head_index + 1) * group_size * HEAD_DIM
    query_head = queries[:, low:high].reshape(row_count, group_size, HEAD_DIM)
    key_head = all_keys[:, head_index * HEAD_DIM : (head_index + 1) * HEAD_DIM]
    logits = (
        jnp.einsum("rhd,kd->rhk", query_head, key_head, preferred_element_type=jnp.float32)
        * scale_factor
    )
    return (query_head, key_head, jnp.where(allowed[:, None, :], logits, NEG_FILL))


def forward(queries, all_keys, all_values, allowed, live_rows, scale_factor):
    row_count = queries.shape[0]
    kv_count = all_keys.shape[1] // HEAD_DIM
    group_size = queries.shape[1] // all_keys.shape[1]
    outputs = []
    totals = []
    for head_index in range(kv_count):
        query_head, key_head, logits = head_logits(
            queries, all_keys, allowed, head_index, group_size, scale_factor
        )
        value_head = all_values[:, head_index * HEAD_DIM : (head_index + 1) * HEAD_DIM]
        row_max = jnp.max(logits, axis=2, keepdims=True)
        log_total = row_max + jnp.log(jnp.sum(jnp.exp(logits - row_max), axis=2, keepdims=True))
        weights = jnp.exp(logits - log_total).astype(jnp.bfloat16)
        mixed = jnp.einsum("rhk,kd->rhd", weights, value_head, preferred_element_type=jnp.float32)
        output_head = jnp.where(live_rows[:, None, None], mixed, 0.0).astype(jnp.bfloat16)
        outputs.append(output_head.reshape(row_count, group_size * HEAD_DIM))
        totals.append(log_total)
    return (jnp.concatenate(outputs, axis=1), totals)


def head_terms(grad_rows, live_rows, output, head_index, group_size):
    row_count = grad_rows.shape[0]
    low = head_index * group_size * HEAD_DIM
    high = (head_index + 1) * group_size * HEAD_DIM
    grad_head = jnp.where(live_rows[:, None], grad_rows[:, low:high], jnp.zeros((), jnp.bfloat16))
    grad_head = grad_head.reshape(row_count, group_size, HEAD_DIM)
    output_head = lax.optimization_barrier(output[:, low:high]).reshape(
        row_count, group_size, HEAD_DIM
    )
    row_dot = jnp.sum(
        grad_head.astype(jnp.float32) * output_head.astype(jnp.float32), axis=2, keepdims=True
    )
    return (grad_head, row_dot)


def backward(
    queries, all_keys, all_values, grad_rows, allowed, live_rows, output, totals, scale_factor
):
    row_count = queries.shape[0]
    kv_count = all_keys.shape[1] // HEAD_DIM
    group_size = queries.shape[1] // all_keys.shape[1]
    query_grads = []
    key_grads = []
    value_grads = []
    for head_index in range(kv_count):
        query_head, key_head, logits = head_logits(
            queries, all_keys, allowed, head_index, group_size, scale_factor
        )
        value_head = all_values[:, head_index * HEAD_DIM : (head_index + 1) * HEAD_DIM]
        prob = jnp.exp(logits - totals[head_index])
        weights = prob.astype(jnp.bfloat16)
        grad_head, row_dot = head_terms(grad_rows, live_rows, output, head_index, group_size)
        spread = jnp.einsum(
            "rhd,kd->rhk", grad_head, value_head, preferred_element_type=jnp.float32
        )
        dlogit = (prob * (spread - row_dot)).astype(jnp.bfloat16)
        query_part = (
            jnp.einsum("rhk,kd->rhd", dlogit, key_head, preferred_element_type=jnp.float32)
            * scale_factor
        )
        query_grads.append(query_part.reshape(row_count, group_size * HEAD_DIM))
        key_grads.append(
            jnp.einsum("rhk,rhd->kd", dlogit, query_head, preferred_element_type=jnp.float32)
            * scale_factor
        )
        value_grads.append(
            jnp.einsum("rhk,rhd->kd", weights, grad_head, preferred_element_type=jnp.float32)
        )
    return (
        jnp.concatenate(query_grads, axis=1),
        jnp.concatenate(key_grads, axis=1),
        jnp.concatenate(value_grads, axis=1),
    )


def collective_body(
    response_query,
    response_key,
    response_value,
    response_grad,
    prompt_key,
    prompt_value,
    lengths,
    home_rank,
    prompt_seen,
):
    rank_count = home_rank.shape[0]
    rank_ids = jnp.arange(rank_count, dtype=jnp.int32)
    resident = jnp.sum(
        jnp.where(home_rank[None, :] == rank_ids[:, None], rank_ids[None, :], 0), axis=1
    )
    own_rank = lax.axis_index("seq")
    scale_factor = 1.0 / HEAD_DIM**0.5
    arrived = (
        lax.all_to_all(response_query[resident], "seq", split_axis=0, concat_axis=1, tiled=True),
        lax.all_to_all(response_key[resident], "seq", split_axis=0, concat_axis=1, tiled=True),
        lax.all_to_all(response_value[resident], "seq", split_axis=0, concat_axis=1, tiled=True),
        lax.all_to_all(response_grad[resident], "seq", split_axis=0, concat_axis=1, tiled=True),
    )
    queries = arrived[0][0]
    own_keys = arrived[1][0]
    own_values = arrived[2][0]
    grad_rows = arrived[3][0]
    own_response = resident[own_rank]
    length = lengths[own_response]
    visible = prompt_seen[own_response]
    max_length = queries.shape[0]
    prompt_rows = prompt_key.shape[0]
    prompt_total = prompt_rows * lax.axis_size("seq")
    positions = jnp.arange(max_length, dtype=jnp.int32)
    prompt_cols = jnp.arange(prompt_total, dtype=jnp.int32)
    seen_part = jnp.broadcast_to(prompt_cols[None, :] < visible, (max_length, prompt_total))
    allowed = jnp.concatenate([seen_part, positions[None, :] <= positions[:, None]], axis=1)
    live_rows = positions < length
    gathered_keys, gathered_values = (
        lax.all_gather(prompt_key, "seq", axis=0, tiled=True),
        lax.all_gather(prompt_value, "seq", axis=0, tiled=True),
    )
    all_keys = jnp.concatenate([gathered_keys, own_keys], axis=0)
    all_values = jnp.concatenate([gathered_values, own_values], axis=0)
    response_out, response_totals = forward(
        queries, all_keys, all_values, allowed, live_rows, scale_factor
    )
    query_grad, key_grad, value_grad = backward(
        queries,
        all_keys,
        all_values,
        grad_rows,
        allowed,
        live_rows,
        response_out,
        response_totals,
        scale_factor,
    )
    key_summed, value_summed = (
        lax.psum_scatter(key_grad[:prompt_total], "seq", scatter_dimension=0, tiled=True),
        lax.psum_scatter(value_grad[:prompt_total], "seq", scatter_dimension=0, tiled=True),
    )
    returned = (
        lax.all_to_all(
            query_grad.astype(jnp.bfloat16)[None], "seq", split_axis=1, concat_axis=0, tiled=True
        ),
        lax.all_to_all(
            key_grad[prompt_total:].astype(jnp.bfloat16)[None],
            "seq",
            split_axis=1,
            concat_axis=0,
            tiled=True,
        ),
        lax.all_to_all(
            value_grad[prompt_total:].astype(jnp.bfloat16)[None],
            "seq",
            split_axis=1,
            concat_axis=0,
            tiled=True,
        ),
    )
    return (
        response_out[None],
        returned[0][home_rank],
        returned[1][home_rank],
        returned[2][home_rank],
        key_summed.astype(jnp.bfloat16),
        value_summed.astype(jnp.bfloat16),
    )


ROW_TILE = 16
VMEM_BYTES = 64 * 1024 * 1024 - 256 * 1024
MESH = pl.DeviceIdType.MESH


def dot_last(left, right):
    return lax.dot_general(left, right, (((1,), (1,)), ((), ())), preferred_element_type=jnp.float32)


def dot_first(left, right):
    return lax.dot_general(left, right, (((0,), (0,)), ((), ())), preferred_element_type=jnp.float32)


def dot_plain(left, right):
    return lax.dot_general(left, right, (((1,), (0,)), ((), ())), preferred_element_type=jnp.float32)


def wait_bytes(ref, sem):
    pltpu.make_async_copy(ref, ref, sem).wait()


def kernel(
    n, inner, prompt_rows,
    q_hbm, k_hbm, v_hbm, g_hbm, pk_hbm, pv_hbm, len_hbm, home_hbm, seen_hbm,
    out_ref, back_q, dk_hbm, dv_hbm, dpk_hbm, dpv_hbm,
    q_ref, k_ref, v_ref, g_ref, len_ref, home_ref, seen_ref,
    pk_ref, pv_ref, dk_ref, dv_ref, dpk_ref, dpv_ref,
    send_qg, send_kv, send_p, in_qg, in_kv, in_p,
    out_send, grad_q, grad_kv, grad_p, back_kv, back_p, acc,
    sem_load, sem_local, sem_send, sem_kv_out, sem_grad_out,
    sem_p, sem_qg, sem_kv, sem_out, sem_q, sem_grad, sem_gp,
):
    me = lax.axis_index("seq")
    outer = n // inner
    mz, mx = lax.div(me, inner), lax.rem(me, inner)
    rows, width = q_ref.shape[1:]
    kv_width = k_ref.shape[2]
    kv_heads = kv_width // HEAD_DIM
    group = width // kv_width
    total = n * rows
    block = inner * rows
    stacked = group * block
    slot = in_p.shape[0] // n
    scale = 1.0 / HEAD_DIM**0.5

    loads = [
        pltpu.make_async_copy(src, dst, sem_load.at[i])
        for i, (src, dst) in enumerate((
            (len_hbm, len_ref), (home_hbm, home_ref), (seen_hbm, seen_ref),
            (k_hbm, k_ref), (v_hbm, v_ref), (pk_hbm, pk_ref), (pv_hbm, pv_ref),
            (q_hbm, q_ref), (g_hbm, g_ref),
        ))
    ]
    for load in loads:
        load.start()
    in_kv[...] = jnp.zeros_like(in_kv)
    back_kv[...] = jnp.zeros_like(back_kv)
    barrier = pltpu.get_barrier_semaphore()
    for step in range(1, n):
        pl.semaphore_signal(
            barrier, inc=1, device_id={"seq": lax.rem(me + step, n)}, device_id_type=MESH
        )

    def send(src, dst, send_sem, recv_sem, peer):
        pltpu.make_async_remote_copy(
            src_ref=src, dst_ref=dst, send_sem=send_sem, recv_sem=recv_sem,
            device_id={"seq": peer}, device_id_type=MESH,
        ).start()

    def tile(index, size):
        return pl.ds(pl.multiple_of(index * size, size), size)

    def pair_cols(head):
        return head * 2 * HEAD_DIM, head * 2 * HEAD_DIM + HEAD_DIM

    for load in loads[:7]:
        load.wait()
    prompt_pad = jnp.zeros((slot - prompt_rows, HEAD_DIM), jnp.float32)
    for h in range(kv_heads):
        kc, vc = pair_cols(h)
        own = slice(h * HEAD_DIM, (h + 1) * HEAD_DIM)
        for ref, col in ((pk_ref, kc), (pv_ref, vc)):
            part = ref[:, own].astype(jnp.float32)
            if slot > prompt_rows:
                part = jnp.concatenate([part, prompt_pad], axis=0)
            send_p[:, col : col + HEAD_DIM] = part.astype(jnp.bfloat16)

    def resident(rank):
        found = jnp.int32(0)
        for r in range(n):
            found = jnp.where(home_ref[r] == rank, jnp.int32(r), found)
        return found

    sources = [resident(rank) for rank in range(n)]
    for rank in range(n):
        key_rows = k_ref[sources[rank]]
        value_rows = v_ref[sources[rank]]
        for h in range(kv_heads):
            kc, vc = pair_cols(h)
            own = slice(h * HEAD_DIM, (h + 1) * HEAD_DIM)
            send_kv[rank, :, kc : kc + HEAD_DIM] = key_rows[:, own]
            send_kv[rank, :, vc : vc + HEAD_DIM] = value_rows[:, own]
    pl.semaphore_wait(barrier, n - 1)

    partner = mz * inner + (inner - 1 - mx)
    own_rows = tile(me, rows)

    def send_keys(stage):
        for step in range(outer):
            @pl.when(mz + step < outer)
            def _():
                for dx in range(inner):
                    home = stage * inner + dx
                    peer = (mz + step) * inner + dx

                    def go():
                        send(send_kv.at[home], in_kv.at[stage, own_rows, :],
                             sem_kv_out.at[step], sem_kv.at[stage, mz], peer)

                    if step == 0:
                        pl.when(mx != dx)(go)
                    else:
                        go()

    head_width = group * HEAD_DIM

    def send_rows(unit):
        stage, h = unit // kv_heads, unit % kv_heads
        cols = pl.ds(h * head_width, head_width)
        send(send_qg.at[stage * inner + inner - 1 - mx, :, :, cols],
             in_qg.at[stage, :, tile(mx, rows), cols],
             sem_send.at[1], sem_qg.at[unit], partner)

    units = outer * kv_heads
    lead = 2
    send_keys(0)
    for step in range(1, n):
        send(send_p, in_p.at[tile(me, slot), :], sem_send.at[0], sem_p, lax.rem(me + step, n))
    loads[7].wait()
    loads[8].wait()
    for stage in range(outer):
        for dx in range(inner):
            rank = stage * inner + dx
            send_qg[rank, 0] = q_ref[sources[rank]]
            send_qg[rank, 1] = g_ref[sources[rank]]
        for unit in range(stage * kv_heads, (stage + 1) * kv_heads):
            if unit < lead:
                send_rows(unit)
        in_qg[stage, :, tile(mx, rows), :] = send_qg[stage * inner + mx]
        in_kv[stage, own_rows, :] = send_kv[stage * inner + mx]
    in_p[tile(me, slot), :] = send_p[...]

    keys_total = total + n * slot
    row_id = lax.broadcasted_iota(jnp.int32, (stacked, keys_total), 0)
    position = mz * block + row_id - (row_id // block) * block
    col_id = lax.broadcasted_iota(jnp.int32, (stacked, keys_total), 1)
    in_prompt = col_id - total
    prompt_slot = in_prompt // slot
    prompt_row = in_prompt - prompt_slot * slot
    prompt_id = prompt_slot * prompt_rows + prompt_row
    far = jnp.int32(2**30)
    prompt_rank = jnp.where(prompt_row < prompt_rows, prompt_id, far)
    ahead = col_id - position
    live_row = lax.broadcasted_iota(jnp.int32, (stacked, HEAD_DIM), 0)
    live_position = mz * block + live_row - (live_row // block) * block

    wait_bytes(in_p.at[0 : (n - 1) * slot, :], sem_p)
    acc[...] = jnp.zeros_like(acc)
    for stage in range(outer):
        home = stage * inner + mx
        source = resident(home)
        length = len_ref[source]
        visible = seen_ref[source]
        allowed = jnp.where(col_id < total, ahead, prompt_rank - visible + 1) <= 0
        live = live_position < length
        for step in range(outer):
            @pl.when(step < mz)
            def _():
                wait_bytes(in_kv.at[stage, 0:block, :], sem_kv.at[stage, step])

            @pl.when(step == mz)
            def _():
                wait_bytes(in_kv.at[stage, 0:rows, :], sem_kv.at[stage, step])
        if stage + 1 < outer:
            send_keys(stage + 1)
        for h in range(kv_heads):
            unit = stage * kv_heads + h
            cols = pl.ds(h * head_width, head_width)
            wait_bytes(in_qg.at[stage, :, 0:rows, cols], sem_qg.at[unit])
            if unit + lead < units:
                send_rows(unit + lead)
            kc, vc = pair_cols(h)
            keys = jnp.concatenate(
                [in_kv[stage, :, kc : kc + HEAD_DIM], in_p[:, kc : kc + HEAD_DIM]], axis=0
            )
            values = jnp.concatenate(
                [in_kv[stage, :, vc : vc + HEAD_DIM], in_p[:, vc : vc + HEAD_DIM]], axis=0
            )
            heads = [
                slice((h * group + a) * HEAD_DIM, (h * group + a + 1) * HEAD_DIM)
                for a in range(group)
            ]
            query = jnp.concatenate([in_qg[stage, 0, :, c] for c in heads], axis=0)
            grad = jnp.concatenate([in_qg[stage, 1, :, c] for c in heads], axis=0)
            grad_wide = jnp.where(live, grad.astype(jnp.float32), 0.0)
            grad = grad_wide.astype(jnp.bfloat16)
            logits = jnp.where(allowed, dot_last(query, keys) * scale, NEG_FILL)
            exped = jnp.exp(logits - jnp.max(logits, axis=1, keepdims=True))
            prob = exped * (1.0 / jnp.sum(exped, axis=1, keepdims=True))
            weights = prob.astype(jnp.bfloat16)
            output = jnp.where(live, dot_plain(weights, values), 0.0).astype(jnp.bfloat16)
            row_dot = jnp.sum(grad_wide * output.astype(jnp.float32), axis=1, keepdims=True)
            dlogit = (prob * (dot_last(grad, values) - row_dot)).astype(jnp.bfloat16)
            dquery = (dot_plain(dlogit, keys) * scale).astype(jnp.bfloat16)
            for a in range(group):
                part = slice(a * block, (a + 1) * block)
                out_send[stage, :, heads[a]] = output[part]
                grad_q[stage, :, heads[a]] = dquery[part]
            dkey = dot_first(dlogit, query) * scale
            dvalue = dot_first(weights, grad)
            for col, part in ((kc, dkey), (vc, dvalue)):
                grad_kv[stage, :, col : col + HEAD_DIM] = part[:total].astype(jnp.bfloat16)
                acc[:, col : col + HEAD_DIM] += part[total:]

            @pl.when(mz != stage)
            def _():
                send(out_send.at[stage, :, cols], out_ref.at[0, tile(mz, block), cols],
                     sem_send.at[2], sem_out, home)

            @pl.when(mz == stage)
            def _():
                pltpu.make_async_copy(
                    out_send.at[stage, :, cols], out_ref.at[0, tile(mz, block), cols], sem_local.at[0]
                ).start()

            send(grad_q.at[stage, tile(inner - 1 - mx, rows), cols], back_q.at[home, :, cols],
                 sem_send.at[3], sem_q, partner)
            pltpu.make_async_copy(
                grad_q.at[stage, tile(mx, rows), cols], back_q.at[home, :, cols], sem_local.at[1]
            ).start()

        for step in range(outer):
            @pl.when(mz - step >= 0)
            def _():
                for dx in range(inner):
                    chunk = (mz - step) * inner + dx

                    def go():
                        send(grad_kv.at[stage, tile(chunk, rows), :], back_kv.at[mz, home],
                             sem_grad_out.at[step], sem_grad.at[mz], chunk)

                    if step == 0:
                        pl.when(mx != dx)(go)
                    else:
                        go()
        back_kv[mz, home] = grad_kv[stage, own_rows, :]
    grad_p[...] = acc[...].astype(jnp.bfloat16)
    for step in range(1, n):
        peer = lax.rem(me + step, n)
        send(grad_p.at[tile(peer, slot), :], back_p.at[me], sem_send.at[4], sem_gp, peer)
    back_p[me] = grad_p[tile(me, slot), :]

    for step in range(outer):
        @pl.when(step > mz)
        def _():
            wait_bytes(back_kv.at[step], sem_grad.at[step])

        @pl.when(step == mz)
        def _():
            wait_bytes(back_kv.at[step, 0:outer], sem_grad.at[step])
    for r in range(n):
        home = home_ref[r]
        summed = back_kv[0, home].astype(jnp.float32)
        for step in range(1, outer):
            summed = summed + back_kv[step, home].astype(jnp.float32)
        summed = summed.astype(jnp.bfloat16)
        for h in range(kv_heads):
            kc, vc = pair_cols(h)
            own = slice(h * HEAD_DIM, (h + 1) * HEAD_DIM)
            dk_ref[r, :, own] = summed[:, kc : kc + HEAD_DIM]
            dv_ref[r, :, own] = summed[:, vc : vc + HEAD_DIM]
    wait_bytes(back_p.at[0 : n - 1], sem_gp)
    prompt_sum = back_p[0].astype(jnp.float32)
    for rank in range(1, n):
        prompt_sum = prompt_sum + back_p[rank].astype(jnp.float32)
    for h in range(kv_heads):
        kc, vc = pair_cols(h)
        own = slice(h * HEAD_DIM, (h + 1) * HEAD_DIM)
        dpk_ref[:, own] = prompt_sum[:prompt_rows, kc : kc + HEAD_DIM].astype(jnp.bfloat16)
        dpv_ref[:, own] = prompt_sum[:prompt_rows, vc : vc + HEAD_DIM].astype(jnp.bfloat16)

    stores = [
        pltpu.make_async_copy(src, dst, sem_load.at[i])
        for i, (src, dst) in enumerate((
            (dk_ref, dk_hbm), (dv_ref, dv_hbm), (dpk_ref, dpk_hbm), (dpv_ref, dpv_hbm),
        ))
    ]
    for store in stores:
        store.start()
    wait_bytes(out_send.at[0], sem_local.at[0])
    wait_bytes(back_q.at[0:outer], sem_local.at[1])
    wait_bytes(out_send.at[0 : outer - 1], sem_out)
    wait_bytes(back_q.at[0:outer], sem_q)
    wait_bytes(back_p.at[0 : n - 1], sem_send.at[0])
    wait_bytes(in_qg.at[:, :, 0:rows, :], sem_send.at[1])
    wait_bytes(out_send.at[0 : outer - 1], sem_send.at[2])
    wait_bytes(back_q.at[0:outer], sem_send.at[3])
    wait_bytes(back_p.at[0 : n - 1], sem_send.at[4])
    for sem in (sem_kv_out, sem_grad_out):
        for step in range(outer):
            reached = mz + step < outer if sem is sem_kv_out else mz - step >= 0

            @pl.when(reached)
            def _():
                wait_bytes(send_kv.at[0 : outer if step == 0 else n], sem.at[step])
    for store in stores:
        store.wait()


def place_kernel(n, *refs):
    sources, home_hbm = refs[:6], refs[6]
    results, held, home_ref = refs[7:13], refs[13:19], refs[19]
    sem_in, sem_out, sem_row, sem_home = refs[20:]
    ranks = pltpu.make_async_copy(home_hbm, home_ref, sem_home)
    ranks.start()
    reads = [
        pltpu.make_async_copy(src, dst, sem_in.at[i]) for i, (src, dst) in enumerate(zip(sources, held))
    ]
    for copy in reads:
        copy.start()
    writes = []
    for i in (0, 2, 3, 4, 5):
        reads[i].wait()
        writes.append(pltpu.make_async_copy(held[i], results[i], sem_out.at[i]))
        writes[-1].start()
    reads[1].wait()
    ranks.wait()
    for r in range(n):
        writes.append(pltpu.make_async_copy(held[1].at[home_ref[r]], results[1].at[r], sem_row.at[r]))
        writes[-1].start()
    for copy in writes:
        copy.wait()


def kernel_body(*arrays):
    query, key, _, _, prompt_key, _, lengths, home_rank, _ = arrays
    n = lax.axis_size("seq")
    inner = 2
    outer = n // inner
    rows, width = query.shape[1:]
    kv_width = key.shape[2]
    prompt_rows = prompt_key.shape[0]
    slot = -(-prompt_rows // ROW_TILE) * ROW_TILE
    total = n * rows
    bf16 = jnp.bfloat16
    hbm = pl.BlockSpec(memory_space=pltpu.HBM)
    shapes = (
        jax.ShapeDtypeStruct((1, total, width), bf16),
        jax.ShapeDtypeStruct(query.shape, bf16),
        jax.ShapeDtypeStruct(key.shape, bf16),
        jax.ShapeDtypeStruct(key.shape, bf16),
        jax.ShapeDtypeStruct(prompt_key.shape, bf16),
        jax.ShapeDtypeStruct(prompt_key.shape, bf16),
    )
    dma = pltpu.SemaphoreType.DMA
    results = pl.pallas_call(
        functools.partial(kernel, n, inner, prompt_rows),
        out_shape=shapes,
        in_specs=[hbm] * 9,
        out_specs=(hbm,) * 6,
        scratch_shapes=[
            pltpu.VMEM(query.shape, bf16),
            pltpu.VMEM(key.shape, bf16),
            pltpu.VMEM(key.shape, bf16),
            pltpu.VMEM(query.shape, bf16),
            pltpu.SMEM(lengths.shape, jnp.int32),
            pltpu.SMEM(lengths.shape, jnp.int32),
            pltpu.SMEM(lengths.shape, jnp.int32),
            pltpu.VMEM(prompt_key.shape, bf16),
            pltpu.VMEM(prompt_key.shape, bf16),
            *(pltpu.VMEM(shape.shape, bf16) for shape in shapes[2:]),
            pltpu.VMEM((n, 2, rows, width), bf16),
            pltpu.VMEM((n, rows, 2 * kv_width), bf16),
            pltpu.VMEM((slot, 2 * kv_width), bf16),
            pltpu.VMEM((outer, 2, inner * rows, width), bf16),
            pltpu.VMEM((outer, total, 2 * kv_width), bf16),
            pltpu.VMEM((n * slot, 2 * kv_width), bf16),
            pltpu.VMEM((outer, inner * rows, width), bf16),
            pltpu.VMEM((outer, inner * rows, width), bf16),
            pltpu.VMEM((outer, total, 2 * kv_width), bf16),
            pltpu.VMEM((n * slot, 2 * kv_width), bf16),
            pltpu.VMEM((outer, n, rows, 2 * kv_width), bf16),
            pltpu.VMEM((n, slot, 2 * kv_width), bf16),
            pltpu.VMEM((n * slot, 2 * kv_width), jnp.float32),
            dma((9,)), dma((2,)), dma((5,)), dma((outer,)), dma((outer,)),
            dma, dma((outer * (kv_width // HEAD_DIM),)), dma((outer, outer)), dma, dma, dma((outer,)), dma,
        ],
        compiler_params=pltpu.CompilerParams(
            collective_id=0, has_side_effects=True, vmem_limit_bytes=VMEM_BYTES
        ),
    )(*arrays)
    return pl.pallas_call(
        functools.partial(place_kernel, n),
        out_shape=shapes,
        in_specs=[hbm] * 7,
        out_specs=(hbm,) * 6,
        scratch_shapes=[
            *(pltpu.VMEM(shape.shape, bf16) for shape in shapes),
            pltpu.SMEM(home_rank.shape, jnp.int32),
            dma((6,)), dma((6,)), dma((n,)), dma,
        ],
        compiler_params=pltpu.CompilerParams(vmem_limit_bytes=VMEM_BYTES),
    )(*results, home_rank)


def body(*arrays):
    rows = arrays[0].shape[1]
    slot = -(-arrays[4].shape[0] // ROW_TILE) * ROW_TILE
    if rows % ROW_TILE == 0 and slot == rows and lax.axis_size("seq") % 2 == 0:
        return kernel_body(*arrays)
    return collective_body(*arrays)


def solution(mesh):
    placed = (
        P("group", "seq", "head"),
        P("group", "seq", "head"),
        P("group", "seq", "head"),
        P("group", "seq", "head"),
        P(("group", "seq"), "head"),
        P(("group", "seq"), "head"),
        P("group"),
        P("group"),
        P("group"),
    )
    return jax.shard_map(
        body,
        mesh=mesh,
        in_specs=placed,
        out_specs=(
            P(("group", "seq"), None, "head"),
            P("group", "seq", "head"),
            P("group", "seq", "head"),
            P("group", "seq", "head"),
            P(("group", "seq"), "head"),
            P(("group", "seq"), "head"),
        ),
        check_vma=False,
    )
```

```python
import functools

import jax
import jax.numpy as jnp
from jax import lax
from jax.experimental import pallas as pl
from jax.experimental.pallas import tpu as pltpu
from jax.sharding import PartitionSpec as P

HEAD_DIM = 128


NEG_FILL = -1e30


def head_logits(queries, all_keys, allowed, head_index, group_size, scale_factor):
    row_count = queries.shape[0]
    low = head_index * group_size * HEAD_DIM
    high = (head_index + 1) * group_size * HEAD_DIM
    query_head = queries[:, low:high].reshape(row_count, group_size, HEAD_DIM)
    key_head = all_keys[:, head_index * HEAD_DIM : (head_index + 1) * HEAD_DIM]
    logits = (
        jnp.einsum("rhd,kd->rhk", query_head, key_head, preferred_element_type=jnp.float32)
        * scale_factor
    )
    return (query_head, key_head, jnp.where(allowed[:, None, :], logits, NEG_FILL))


def forward(queries, all_keys, all_values, allowed, live_rows, scale_factor):
    row_count = queries.shape[0]
    kv_count = all_keys.shape[1] // HEAD_DIM
    group_size = queries.shape[1] // all_keys.shape[1]
    outputs = []
    totals = []
    for head_index in range(kv_count):
        query_head, key_head, logits = head_logits(
            queries, all_keys, allowed, head_index, group_size, scale_factor
        )
        value_head = all_values[:, head_index * HEAD_DIM : (head_index + 1) * HEAD_DIM]
        row_max = jnp.max(logits, axis=2, keepdims=True)
        log_total = row_max + jnp.log(jnp.sum(jnp.exp(logits - row_max), axis=2, keepdims=True))
        weights = jnp.exp(logits - log_total).astype(jnp.bfloat16)
        mixed = jnp.einsum("rhk,kd->rhd", weights, value_head, preferred_element_type=jnp.float32)
        output_head = jnp.where(live_rows[:, None, None], mixed, 0.0).astype(jnp.bfloat16)
        outputs.append(output_head.reshape(row_count, group_size * HEAD_DIM))
        totals.append(log_total)
    return (jnp.concatenate(outputs, axis=1), totals)


def head_terms(grad_rows, live_rows, output, head_index, group_size):
    row_count = grad_rows.shape[0]
    low = head_index * group_size * HEAD_DIM
    high = (head_index + 1) * group_size * HEAD_DIM
    grad_head = jnp.where(live_rows[:, None], grad_rows[:, low:high], jnp.zeros((), jnp.bfloat16))
    grad_head = grad_head.reshape(row_count, group_size, HEAD_DIM)
    output_head = lax.optimization_barrier(output[:, low:high]).reshape(
        row_count, group_size, HEAD_DIM
    )
    row_dot = jnp.sum(
        grad_head.astype(jnp.float32) * output_head.astype(jnp.float32), axis=2, keepdims=True
    )
    return (grad_head, row_dot)


def backward(
    queries, all_keys, all_values, grad_rows, allowed, live_rows, output, totals, scale_factor
):
    row_count = queries.shape[0]
    kv_count = all_keys.shape[1] // HEAD_DIM
    group_size = queries.shape[1] // all_keys.shape[1]
    query_grads = []
    key_grads = []
    value_grads = []
    for head_index in range(kv_count):
        query_head, key_head, logits = head_logits(
            queries, all_keys, allowed, head_index, group_size, scale_factor
        )
        value_head = all_values[:, head_index * HEAD_DIM : (head_index + 1) * HEAD_DIM]
        prob = jnp.exp(logits - totals[head_index])
        weights = prob.astype(jnp.bfloat16)
        grad_head, row_dot = head_terms(grad_rows, live_rows, output, head_index, group_size)
        spread = jnp.einsum(
            "rhd,kd->rhk", grad_head, value_head, preferred_element_type=jnp.float32
        )
        dlogit = (prob * (spread - row_dot)).astype(jnp.bfloat16)
        query_part = (
            jnp.einsum("rhk,kd->rhd", dlogit, key_head, preferred_element_type=jnp.float32)
            * scale_factor
        )
        query_grads.append(query_part.reshape(row_count, group_size * HEAD_DIM))
        key_grads.append(
            jnp.einsum("rhk,rhd->kd", dlogit, query_head, preferred_element_type=jnp.float32)
            * scale_factor
        )
        value_grads.append(
            jnp.einsum("rhk,rhd->kd", weights, grad_head, preferred_element_type=jnp.float32)
        )
    return (
        jnp.concatenate(query_grads, axis=1),
        jnp.concatenate(key_grads, axis=1),
        jnp.concatenate(value_grads, axis=1),
    )


def collective_body(
    response_query,
    response_key,
    response_value,
    response_grad,
    prompt_key,
    prompt_value,
    lengths,
    home_rank,
    prompt_seen,
):
    rank_count = home_rank.shape[0]
    rank_ids = jnp.arange(rank_count, dtype=jnp.int32)
    resident = jnp.sum(
        jnp.where(home_rank[None, :] == rank_ids[:, None], rank_ids[None, :], 0), axis=1
    )
    own_rank = lax.axis_index("seq")
    scale_factor = 1.0 / HEAD_DIM**0.5
    arrived = (
        lax.all_to_all(response_query[resident], "seq", split_axis=0, concat_axis=1, tiled=True),
        lax.all_to_all(response_key[resident], "seq", split_axis=0, concat_axis=1, tiled=True),
        lax.all_to_all(response_value[resident], "seq", split_axis=0, concat_axis=1, tiled=True),
        lax.all_to_all(response_grad[resident], "seq", split_axis=0, concat_axis=1, tiled=True),
    )
    queries = arrived[0][0]
    own_keys = arrived[1][0]
    own_values = arrived[2][0]
    grad_rows = arrived[3][0]
    own_response = resident[own_rank]
    length = lengths[own_response]
    visible = prompt_seen[own_response]
    max_length = queries.shape[0]
    prompt_rows = prompt_key.shape[0]
    prompt_total = prompt_rows * lax.axis_size("seq")
    positions = jnp.arange(max_length, dtype=jnp.int32)
    prompt_cols = jnp.arange(prompt_total, dtype=jnp.int32)
    seen_part = jnp.broadcast_to(prompt_cols[None, :] < visible, (max_length, prompt_total))
    allowed = jnp.concatenate([seen_part, positions[None, :] <= positions[:, None]], axis=1)
    live_rows = positions < length
    gathered_keys, gathered_values = (
        lax.all_gather(prompt_key, "seq", axis=0, tiled=True),
        lax.all_gather(prompt_value, "seq", axis=0, tiled=True),
    )
    all_keys = jnp.concatenate([gathered_keys, own_keys], axis=0)
    all_values = jnp.concatenate([gathered_values, own_values], axis=0)
    response_out, response_totals = forward(
        queries, all_keys, all_values, allowed, live_rows, scale_factor
    )
    query_grad, key_grad, value_grad = backward(
        queries,
        all_keys,
        all_values,
        grad_rows,
        allowed,
        live_rows,
        response_out,
        response_totals,
        scale_factor,
    )
    key_summed, value_summed = (
        lax.psum_scatter(key_grad[:prompt_total], "seq", scatter_dimension=0, tiled=True),
        lax.psum_scatter(value_grad[:prompt_total], "seq", scatter_dimension=0, tiled=True),
    )
    returned = (
        lax.all_to_all(
            query_grad.astype(jnp.bfloat16)[None], "seq", split_axis=1, concat_axis=0, tiled=True
        ),
        lax.all_to_all(
            key_grad[prompt_total:].astype(jnp.bfloat16)[None],
            "seq",
            split_axis=1,
            concat_axis=0,
            tiled=True,
        ),
        lax.all_to_all(
            value_grad[prompt_total:].astype(jnp.bfloat16)[None],
            "seq",
            split_axis=1,
            concat_axis=0,
            tiled=True,
        ),
    )
    return (
        response_out[None],
        returned[0][home_rank],
        returned[1][home_rank],
        returned[2][home_rank],
        key_summed.astype(jnp.bfloat16),
        value_summed.astype(jnp.bfloat16),
    )


ROW_TILE = 16
LOG2E = 1.4426950408889634
VMEM_BYTES = 64 * 1024 * 1024 - 256 * 1024
MESH = pl.DeviceIdType.MESH


def dot_last(left, right):
    return lax.dot_general(left, right, (((1,), (1,)), ((), ())), preferred_element_type=jnp.float32)


def dot_first(left, right):
    return lax.dot_general(left, right, (((0,), (0,)), ((), ())), preferred_element_type=jnp.float32)


def dot_plain(left, right):
    return lax.dot_general(left, right, (((1,), (0,)), ((), ())), preferred_element_type=jnp.float32)


def wait_bytes(ref, sem):
    pltpu.make_async_copy(ref, ref, sem).wait()


def kernel(
    n, inner, prompt_rows,
    q_hbm, k_hbm, v_hbm, g_hbm, pk_hbm, pv_hbm, len_hbm, home_hbm, seen_hbm,
    out_ref, back_q, dk_hbm, dv_hbm, dpk_hbm, dpv_hbm,
    q_ref, k_ref, v_ref, g_ref, len_ref, home_ref, seen_ref,
    pk_ref, pv_ref, dk_ref, dv_ref, dpk_ref, dpv_ref,
    send_qg, send_kv, send_p, in_qg, in_kv, in_p,
    out_send, grad_q, grad_kv, grad_p, back_kv, back_p, acc,
    sem_load, sem_local, sem_send, sem_kv_out, sem_grad_out,
    sem_p, sem_qg, sem_kv, sem_out, sem_q, sem_grad, sem_gp,
):
    me = lax.axis_index("seq")
    outer = n // inner
    mz, mx = lax.div(me, inner), lax.rem(me, inner)
    rows, width = q_ref.shape[1:]
    kv_width = k_ref.shape[2]
    kv_heads = kv_width // HEAD_DIM
    group = width // kv_width
    total = n * rows
    block = inner * rows
    stacked = group * block
    slot = in_p.shape[0] // n
    scale = 1.0 / HEAD_DIM**0.5

    loads = [
        pltpu.make_async_copy(src, dst, sem_load.at[i])
        for i, (src, dst) in enumerate((
            (len_hbm, len_ref), (home_hbm, home_ref), (seen_hbm, seen_ref),
            (k_hbm, k_ref), (v_hbm, v_ref), (pk_hbm, pk_ref), (pv_hbm, pv_ref),
            (q_hbm, q_ref), (g_hbm, g_ref),
        ))
    ]
    for load in loads:
        load.start()
    in_kv[...] = jnp.zeros_like(in_kv)
    back_kv[...] = jnp.zeros_like(back_kv)
    barrier = pltpu.get_barrier_semaphore()
    for step in range(1, n):
        pl.semaphore_signal(
            barrier, inc=1, device_id={"seq": lax.rem(me + step, n)}, device_id_type=MESH
        )

    def send(src, dst, send_sem, recv_sem, peer):
        pltpu.make_async_remote_copy(
            src_ref=src, dst_ref=dst, send_sem=send_sem, recv_sem=recv_sem,
            device_id={"seq": peer}, device_id_type=MESH,
        ).start()

    def tile(index, size):
        return pl.ds(pl.multiple_of(index * size, size), size)

    def pair_cols(head):
        return head * 2 * HEAD_DIM, head * 2 * HEAD_DIM + HEAD_DIM

    for load in loads[:7]:
        load.wait()
    prompt_pad = jnp.zeros((slot - prompt_rows, HEAD_DIM), jnp.float32)
    for h in range(kv_heads):
        kc, vc = pair_cols(h)
        own = slice(h * HEAD_DIM, (h + 1) * HEAD_DIM)
        for ref, col in ((pk_ref, kc), (pv_ref, vc)):
            part = ref[:, own].astype(jnp.float32)
            if slot > prompt_rows:
                part = jnp.concatenate([part, prompt_pad], axis=0)
            send_p[:, col : col + HEAD_DIM] = part.astype(jnp.bfloat16)

    def resident(rank):
        found = jnp.int32(0)
        for r in range(n):
            found = jnp.where(home_ref[r] == rank, jnp.int32(r), found)
        return found

    sources = [resident(rank) for rank in range(n)]
    for rank in range(n):
        key_rows = k_ref[sources[rank]]
        value_rows = v_ref[sources[rank]]
        for h in range(kv_heads):
            kc, vc = pair_cols(h)
            own = slice(h * HEAD_DIM, (h + 1) * HEAD_DIM)
            send_kv[rank, :, kc : kc + HEAD_DIM] = key_rows[:, own]
            send_kv[rank, :, vc : vc + HEAD_DIM] = value_rows[:, own]
    pl.semaphore_wait(barrier, n - 1)

    partner = mz * inner + (inner - 1 - mx)
    own_rows = tile(me, rows)

    def send_keys(stage):
        for step in range(outer):
            @pl.when(mz + step < outer)
            def _():
                for dx in range(inner):
                    home = stage * inner + dx
                    peer = (mz + step) * inner + dx

                    def go():
                        send(send_kv.at[home], in_kv.at[stage, own_rows, :],
                             sem_kv_out.at[step], sem_kv.at[stage, mz], peer)

                    if step == 0:
                        pl.when(mx != dx)(go)
                    else:
                        go()

    head_width = group * HEAD_DIM

    def send_rows(unit):
        stage, h = unit // kv_heads, unit % kv_heads
        cols = pl.ds(h * head_width, head_width)
        send(send_qg.at[stage * inner + inner - 1 - mx, :, :, cols],
             in_qg.at[stage, :, tile(mx, rows), cols],
             sem_send.at[1], sem_qg.at[unit], partner)

    units = outer * kv_heads
    lead = 2
    send_keys(0)
    for step in range(1, n):
        send(send_p, in_p.at[tile(me, slot), :], sem_send.at[0], sem_p, lax.rem(me + step, n))
    loads[7].wait()
    loads[8].wait()
    for stage in range(outer):
        for dx in range(inner):
            rank = stage * inner + dx
            send_qg[rank, 0] = q_ref[sources[rank]]
            send_qg[rank, 1] = g_ref[sources[rank]]
        for unit in range(stage * kv_heads, (stage + 1) * kv_heads):
            if unit < lead:
                send_rows(unit)
        in_qg[stage, :, tile(mx, rows), :] = send_qg[stage * inner + mx]
        in_kv[stage, own_rows, :] = send_kv[stage * inner + mx]
    in_p[tile(me, slot), :] = send_p[...]

    keys_total = total + n * slot
    position = mz * block + lax.broadcasted_iota(jnp.int32, (block, keys_total), 0)
    col_id = lax.broadcasted_iota(jnp.int32, (block, keys_total), 1)
    in_prompt = col_id - total
    prompt_slot = in_prompt // slot
    prompt_row = in_prompt - prompt_slot * slot
    prompt_id = prompt_slot * prompt_rows + prompt_row
    far = jnp.int32(2**30)
    prompt_rank = jnp.where(prompt_row < prompt_rows, prompt_id, far)
    ahead = col_id - position
    live_position = mz * block + lax.broadcasted_iota(jnp.int32, (block, HEAD_DIM), 0)

    def per_head(rows_of_heads, factor, combine):
        shape = rows_of_heads.shape
        return combine(rows_of_heads.reshape(group, block, shape[1]), factor[None]).reshape(shape)

    wait_bytes(in_p.at[0 : (n - 1) * slot, :], sem_p)
    acc[...] = jnp.zeros_like(acc)
    for stage in range(outer):
        home = stage * inner + mx
        source = resident(home)
        length = len_ref[source]
        visible = seen_ref[source]
        allowed = jnp.where(col_id < total, ahead, prompt_rank - visible + 1) <= 0
        bias = jnp.where(allowed, 0.0, NEG_FILL)
        live = (live_position < length).astype(jnp.float32)
        for step in range(outer):
            @pl.when(step < mz)
            def _():
                wait_bytes(in_kv.at[stage, 0:block, :], sem_kv.at[stage, step])

            @pl.when(step == mz)
            def _():
                wait_bytes(in_kv.at[stage, 0:rows, :], sem_kv.at[stage, step])
        if stage + 1 < outer:
            send_keys(stage + 1)
        for h in range(kv_heads):
            unit = stage * kv_heads + h
            cols = pl.ds(h * head_width, head_width)
            wait_bytes(in_qg.at[stage, :, 0:rows, cols], sem_qg.at[unit])
            if unit + lead < units:
                send_rows(unit + lead)
            kc, vc = pair_cols(h)
            keys = jnp.concatenate(
                [in_kv[stage, :, kc : kc + HEAD_DIM], in_p[:, kc : kc + HEAD_DIM]], axis=0
            )
            values = jnp.concatenate(
                [in_kv[stage, :, vc : vc + HEAD_DIM], in_p[:, vc : vc + HEAD_DIM]], axis=0
            )
            heads = [
                slice((h * group + a) * HEAD_DIM, (h * group + a + 1) * HEAD_DIM)
                for a in range(group)
            ]
            query = jnp.concatenate([in_qg[stage, 0, :, c] for c in heads], axis=0)
            grad = jnp.concatenate([in_qg[stage, 1, :, c] for c in heads], axis=0)
            grad_wide = per_head(grad.astype(jnp.float32), live, jnp.multiply)
            grad = grad_wide.astype(jnp.bfloat16)
            logits = per_head(dot_last(query, keys) * (scale * LOG2E), bias, jnp.add)
            exped = jnp.exp2(logits - jnp.max(logits, axis=1, keepdims=True))
            prob = exped * (1.0 / jnp.sum(exped, axis=1, keepdims=True))
            weights = prob.astype(jnp.bfloat16)
            output = per_head(dot_plain(weights, values), live, jnp.multiply).astype(jnp.bfloat16)
            row_dot = jnp.sum(grad_wide * output.astype(jnp.float32), axis=1, keepdims=True)
            dlogit = (prob * (dot_last(grad, values) - row_dot)).astype(jnp.bfloat16)
            dquery = (dot_plain(dlogit, keys) * scale).astype(jnp.bfloat16)
            for a in range(group):
                part = slice(a * block, (a + 1) * block)
                out_send[stage, :, heads[a]] = output[part]
                grad_q[stage, :, heads[a]] = dquery[part]
            dkey = dot_first(dlogit, query) * scale
            dvalue = dot_first(weights, grad)
            for col, part in ((kc, dkey), (vc, dvalue)):
                grad_kv[stage, :, col : col + HEAD_DIM] = part[:total].astype(jnp.bfloat16)
                acc[:, col : col + HEAD_DIM] += part[total:]

            @pl.when(mz != stage)
            def _():
                send(out_send.at[stage, :, cols], out_ref.at[0, tile(mz, block), cols],
                     sem_send.at[2], sem_out, home)

            @pl.when(mz == stage)
            def _():
                pltpu.make_async_copy(
                    out_send.at[stage, :, cols], out_ref.at[0, tile(mz, block), cols], sem_local.at[0]
                ).start()

            send(grad_q.at[stage, tile(inner - 1 - mx, rows), cols], back_q.at[home, :, cols],
                 sem_send.at[3], sem_q, partner)
            pltpu.make_async_copy(
                grad_q.at[stage, tile(mx, rows), cols], back_q.at[home, :, cols], sem_local.at[1]
            ).start()

        for step in range(outer):
            @pl.when(mz - step >= 0)
            def _():
                for dx in range(inner):
                    chunk = (mz - step) * inner + dx

                    def go():
                        send(grad_kv.at[stage, tile(chunk, rows), :], back_kv.at[mz, home],
                             sem_grad_out.at[step], sem_grad.at[mz], chunk)

                    if step == 0:
                        pl.when(mx != dx)(go)
                    else:
                        go()
        back_kv[mz, home] = grad_kv[stage, own_rows, :]
    grad_p[...] = acc[...].astype(jnp.bfloat16)
    for step in range(1, n):
        peer = lax.rem(me + step, n)
        send(grad_p.at[tile(peer, slot), :], back_p.at[me], sem_send.at[4], sem_gp, peer)
    back_p[me] = grad_p[tile(me, slot), :]

    for step in range(outer):
        @pl.when(step > mz)
        def _():
            wait_bytes(back_kv.at[step], sem_grad.at[step])

        @pl.when(step == mz)
        def _():
            wait_bytes(back_kv.at[step, 0:outer], sem_grad.at[step])
    for r in range(n):
        home = home_ref[r]
        summed = back_kv[0, home].astype(jnp.float32)
        for step in range(1, outer):
            summed = summed + back_kv[step, home].astype(jnp.float32)
        summed = summed.astype(jnp.bfloat16)
        for h in range(kv_heads):
            kc, vc = pair_cols(h)
            own = slice(h * HEAD_DIM, (h + 1) * HEAD_DIM)
            dk_ref[r, :, own] = summed[:, kc : kc + HEAD_DIM]
            dv_ref[r, :, own] = summed[:, vc : vc + HEAD_DIM]
    wait_bytes(back_p.at[0 : n - 1], sem_gp)
    prompt_sum = back_p[0].astype(jnp.float32)
    for rank in range(1, n):
        prompt_sum = prompt_sum + back_p[rank].astype(jnp.float32)
    for h in range(kv_heads):
        kc, vc = pair_cols(h)
        own = slice(h * HEAD_DIM, (h + 1) * HEAD_DIM)
        dpk_ref[:, own] = prompt_sum[:prompt_rows, kc : kc + HEAD_DIM].astype(jnp.bfloat16)
        dpv_ref[:, own] = prompt_sum[:prompt_rows, vc : vc + HEAD_DIM].astype(jnp.bfloat16)

    stores = [
        pltpu.make_async_copy(src, dst, sem_load.at[i])
        for i, (src, dst) in enumerate((
            (dk_ref, dk_hbm), (dv_ref, dv_hbm), (dpk_ref, dpk_hbm), (dpv_ref, dpv_hbm),
        ))
    ]
    for store in stores:
        store.start()
    wait_bytes(out_send.at[0], sem_local.at[0])
    wait_bytes(back_q.at[0:outer], sem_local.at[1])
    wait_bytes(out_send.at[0 : outer - 1], sem_out)
    wait_bytes(back_q.at[0:outer], sem_q)
    wait_bytes(back_p.at[0 : n - 1], sem_send.at[0])
    wait_bytes(in_qg.at[:, :, 0:rows, :], sem_send.at[1])
    wait_bytes(out_send.at[0 : outer - 1], sem_send.at[2])
    wait_bytes(back_q.at[0:outer], sem_send.at[3])
    wait_bytes(back_p.at[0 : n - 1], sem_send.at[4])
    for sem in (sem_kv_out, sem_grad_out):
        for step in range(outer):
            reached = mz + step < outer if sem is sem_kv_out else mz - step >= 0

            @pl.when(reached)
            def _():
                wait_bytes(send_kv.at[0 : outer if step == 0 else n], sem.at[step])
    for store in stores:
        store.wait()


def place_kernel(n, *refs):
    sources, home_hbm = refs[:6], refs[6]
    results, held, home_ref = refs[7:13], refs[13:19], refs[19]
    sem_in, sem_out, sem_row, sem_home = refs[20:]
    ranks = pltpu.make_async_copy(home_hbm, home_ref, sem_home)
    ranks.start()
    reads = [
        pltpu.make_async_copy(src, dst, sem_in.at[i]) for i, (src, dst) in enumerate(zip(sources, held))
    ]
    for copy in reads:
        copy.start()
    writes = []
    for i in (0, 2, 3, 4, 5):
        reads[i].wait()
        writes.append(pltpu.make_async_copy(held[i], results[i], sem_out.at[i]))
        writes[-1].start()
    reads[1].wait()
    ranks.wait()
    for r in range(n):
        writes.append(pltpu.make_async_copy(held[1].at[home_ref[r]], results[1].at[r], sem_row.at[r]))
        writes[-1].start()
    for copy in writes:
        copy.wait()


def kernel_body(*arrays):
    query, key, _, _, prompt_key, _, lengths, home_rank, _ = arrays
    n = lax.axis_size("seq")
    inner = 2
    outer = n // inner
    rows, width = query.shape[1:]
    kv_width = key.shape[2]
    prompt_rows = prompt_key.shape[0]
    slot = -(-prompt_rows // ROW_TILE) * ROW_TILE
    total = n * rows
    bf16 = jnp.bfloat16
    hbm = pl.BlockSpec(memory_space=pltpu.HBM)
    shapes = (
        jax.ShapeDtypeStruct((1, total, width), bf16),
        jax.ShapeDtypeStruct(query.shape, bf16),
        jax.ShapeDtypeStruct(key.shape, bf16),
        jax.ShapeDtypeStruct(key.shape, bf16),
        jax.ShapeDtypeStruct(prompt_key.shape, bf16),
        jax.ShapeDtypeStruct(prompt_key.shape, bf16),
    )
    dma = pltpu.SemaphoreType.DMA
    results = pl.pallas_call(
        functools.partial(kernel, n, inner, prompt_rows),
        out_shape=shapes,
        in_specs=[hbm] * 9,
        out_specs=(hbm,) * 6,
        scratch_shapes=[
            pltpu.VMEM(query.shape, bf16),
            pltpu.VMEM(key.shape, bf16),
            pltpu.VMEM(key.shape, bf16),
            pltpu.VMEM(query.shape, bf16),
            pltpu.SMEM(lengths.shape, jnp.int32),
            pltpu.SMEM(lengths.shape, jnp.int32),
            pltpu.SMEM(lengths.shape, jnp.int32),
            pltpu.VMEM(prompt_key.shape, bf16),
            pltpu.VMEM(prompt_key.shape, bf16),
            *(pltpu.VMEM(shape.shape, bf16) for shape in shapes[2:]),
            pltpu.VMEM((n, 2, rows, width), bf16),
            pltpu.VMEM((n, rows, 2 * kv_width), bf16),
            pltpu.VMEM((slot, 2 * kv_width), bf16),
            pltpu.VMEM((outer, 2, inner * rows, width), bf16),
            pltpu.VMEM((outer, total, 2 * kv_width), bf16),
            pltpu.VMEM((n * slot, 2 * kv_width), bf16),
            pltpu.VMEM((outer, inner * rows, width), bf16),
            pltpu.VMEM((outer, inner * rows, width), bf16),
            pltpu.VMEM((outer, total, 2 * kv_width), bf16),
            pltpu.VMEM((n * slot, 2 * kv_width), bf16),
            pltpu.VMEM((outer, n, rows, 2 * kv_width), bf16),
            pltpu.VMEM((n, slot, 2 * kv_width), bf16),
            pltpu.VMEM((n * slot, 2 * kv_width), jnp.float32),
            dma((9,)), dma((2,)), dma((5,)), dma((outer,)), dma((outer,)),
            dma, dma((outer * (kv_width // HEAD_DIM),)), dma((outer, outer)), dma, dma, dma((outer,)), dma,
        ],
        compiler_params=pltpu.CompilerParams(
            collective_id=0, has_side_effects=True, vmem_limit_bytes=VMEM_BYTES
        ),
    )(*arrays)
    return pl.pallas_call(
        functools.partial(place_kernel, n),
        out_shape=shapes,
        in_specs=[hbm] * 7,
        out_specs=(hbm,) * 6,
        scratch_shapes=[
            *(pltpu.VMEM(shape.shape, bf16) for shape in shapes),
            pltpu.SMEM(home_rank.shape, jnp.int32),
            dma((6,)), dma((6,)), dma((n,)), dma,
        ],
        compiler_params=pltpu.CompilerParams(vmem_limit_bytes=VMEM_BYTES),
    )(*results, home_rank)


def body(*arrays):
    rows = arrays[0].shape[1]
    slot = -(-arrays[4].shape[0] // ROW_TILE) * ROW_TILE
    if rows % ROW_TILE == 0 and slot == rows and lax.axis_size("seq") % 2 == 0:
        return kernel_body(*arrays)
    return collective_body(*arrays)


def solution(mesh):
    placed = (
        P("group", "seq", "head"),
        P("group", "seq", "head"),
        P("group", "seq", "head"),
        P("group", "seq", "head"),
        P(("group", "seq"), "head"),
        P(("group", "seq"), "head"),
        P("group"),
        P("group"),
        P("group"),
    )
    return jax.shard_map(
        body,
        mesh=mesh,
        in_specs=placed,
        out_specs=(
            P(("group", "seq"), None, "head"),
            P("group", "seq", "head"),
            P("group", "seq", "head"),
            P("group", "seq", "head"),
            P(("group", "seq"), "head"),
            P(("group", "seq"), "head"),
        ),
        check_vma=False,
    )
```

```python
import functools

import jax
import jax.numpy as jnp
from jax import lax
from jax.experimental import pallas as pl
from jax.experimental.pallas import tpu as pltpu
from jax.sharding import PartitionSpec as P

HEAD_DIM = 128


NEG_FILL = -1e30


def head_logits(queries, all_keys, allowed, head_index, group_size, scale_factor):
    row_count = queries.shape[0]
    low = head_index * group_size * HEAD_DIM
    high = (head_index + 1) * group_size * HEAD_DIM
    query_head = queries[:, low:high].reshape(row_count, group_size, HEAD_DIM)
    key_head = all_keys[:, head_index * HEAD_DIM : (head_index + 1) * HEAD_DIM]
    logits = (
        jnp.einsum("rhd,kd->rhk", query_head, key_head, preferred_element_type=jnp.float32)
        * scale_factor
    )
    return (query_head, key_head, jnp.where(allowed[:, None, :], logits, NEG_FILL))


def forward(queries, all_keys, all_values, allowed, live_rows, scale_factor):
    row_count = queries.shape[0]
    kv_count = all_keys.shape[1] // HEAD_DIM
    group_size = queries.shape[1] // all_keys.shape[1]
    outputs = []
    totals = []
    for head_index in range(kv_count):
        query_head, key_head, logits = head_logits(
            queries, all_keys, allowed, head_index, group_size, scale_factor
        )
        value_head = all_values[:, head_index * HEAD_DIM : (head_index + 1) * HEAD_DIM]
        row_max = jnp.max(logits, axis=2, keepdims=True)
        log_total = row_max + jnp.log(jnp.sum(jnp.exp(logits - row_max), axis=2, keepdims=True))
        weights = jnp.exp(logits - log_total).astype(jnp.bfloat16)
        mixed = jnp.einsum("rhk,kd->rhd", weights, value_head, preferred_element_type=jnp.float32)
        output_head = jnp.where(live_rows[:, None, None], mixed, 0.0).astype(jnp.bfloat16)
        outputs.append(output_head.reshape(row_count, group_size * HEAD_DIM))
        totals.append(log_total)
    return (jnp.concatenate(outputs, axis=1), totals)


def head_terms(grad_rows, live_rows, output, head_index, group_size):
    row_count = grad_rows.shape[0]
    low = head_index * group_size * HEAD_DIM
    high = (head_index + 1) * group_size * HEAD_DIM
    grad_head = jnp.where(live_rows[:, None], grad_rows[:, low:high], jnp.zeros((), jnp.bfloat16))
    grad_head = grad_head.reshape(row_count, group_size, HEAD_DIM)
    output_head = lax.optimization_barrier(output[:, low:high]).reshape(
        row_count, group_size, HEAD_DIM
    )
    row_dot = jnp.sum(
        grad_head.astype(jnp.float32) * output_head.astype(jnp.float32), axis=2, keepdims=True
    )
    return (grad_head, row_dot)


def backward(
    queries, all_keys, all_values, grad_rows, allowed, live_rows, output, totals, scale_factor
):
    row_count = queries.shape[0]
    kv_count = all_keys.shape[1] // HEAD_DIM
    group_size = queries.shape[1] // all_keys.shape[1]
    query_grads = []
    key_grads = []
    value_grads = []
    for head_index in range(kv_count):
        query_head, key_head, logits = head_logits(
            queries, all_keys, allowed, head_index, group_size, scale_factor
        )
        value_head = all_values[:, head_index * HEAD_DIM : (head_index + 1) * HEAD_DIM]
        prob = jnp.exp(logits - totals[head_index])
        weights = prob.astype(jnp.bfloat16)
        grad_head, row_dot = head_terms(grad_rows, live_rows, output, head_index, group_size)
        spread = jnp.einsum(
            "rhd,kd->rhk", grad_head, value_head, preferred_element_type=jnp.float32
        )
        dlogit = (prob * (spread - row_dot)).astype(jnp.bfloat16)
        query_part = (
            jnp.einsum("rhk,kd->rhd", dlogit, key_head, preferred_element_type=jnp.float32)
            * scale_factor
        )
        query_grads.append(query_part.reshape(row_count, group_size * HEAD_DIM))
        key_grads.append(
            jnp.einsum("rhk,rhd->kd", dlogit, query_head, preferred_element_type=jnp.float32)
            * scale_factor
        )
        value_grads.append(
            jnp.einsum("rhk,rhd->kd", weights, grad_head, preferred_element_type=jnp.float32)
        )
    return (
        jnp.concatenate(query_grads, axis=1),
        jnp.concatenate(key_grads, axis=1),
        jnp.concatenate(value_grads, axis=1),
    )


def collective_body(
    response_query,
    response_key,
    response_value,
    response_grad,
    prompt_key,
    prompt_value,
    lengths,
    home_rank,
    prompt_seen,
):
    rank_count = home_rank.shape[0]
    rank_ids = jnp.arange(rank_count, dtype=jnp.int32)
    resident = jnp.sum(
        jnp.where(home_rank[None, :] == rank_ids[:, None], rank_ids[None, :], 0), axis=1
    )
    own_rank = lax.axis_index("seq")
    scale_factor = 1.0 / HEAD_DIM**0.5
    arrived = (
        lax.all_to_all(response_query[resident], "seq", split_axis=0, concat_axis=1, tiled=True),
        lax.all_to_all(response_key[resident], "seq", split_axis=0, concat_axis=1, tiled=True),
        lax.all_to_all(response_value[resident], "seq", split_axis=0, concat_axis=1, tiled=True),
        lax.all_to_all(response_grad[resident], "seq", split_axis=0, concat_axis=1, tiled=True),
    )
    queries = arrived[0][0]
    own_keys = arrived[1][0]
    own_values = arrived[2][0]
    grad_rows = arrived[3][0]
    own_response = resident[own_rank]
    length = lengths[own_response]
    visible = prompt_seen[own_response]
    max_length = queries.shape[0]
    prompt_rows = prompt_key.shape[0]
    prompt_total = prompt_rows * lax.axis_size("seq")
    positions = jnp.arange(max_length, dtype=jnp.int32)
    prompt_cols = jnp.arange(prompt_total, dtype=jnp.int32)
    seen_part = jnp.broadcast_to(prompt_cols[None, :] < visible, (max_length, prompt_total))
    allowed = jnp.concatenate([seen_part, positions[None, :] <= positions[:, None]], axis=1)
    live_rows = positions < length
    gathered_keys, gathered_values = (
        lax.all_gather(prompt_key, "seq", axis=0, tiled=True),
        lax.all_gather(prompt_value, "seq", axis=0, tiled=True),
    )
    all_keys = jnp.concatenate([gathered_keys, own_keys], axis=0)
    all_values = jnp.concatenate([gathered_values, own_values], axis=0)
    response_out, response_totals = forward(
        queries, all_keys, all_values, allowed, live_rows, scale_factor
    )
    query_grad, key_grad, value_grad = backward(
        queries,
        all_keys,
        all_values,
        grad_rows,
        allowed,
        live_rows,
        response_out,
        response_totals,
        scale_factor,
    )
    key_summed, value_summed = (
        lax.psum_scatter(key_grad[:prompt_total], "seq", scatter_dimension=0, tiled=True),
        lax.psum_scatter(value_grad[:prompt_total], "seq", scatter_dimension=0, tiled=True),
    )
    returned = (
        lax.all_to_all(
            query_grad.astype(jnp.bfloat16)[None], "seq", split_axis=1, concat_axis=0, tiled=True
        ),
        lax.all_to_all(
            key_grad[prompt_total:].astype(jnp.bfloat16)[None],
            "seq",
            split_axis=1,
            concat_axis=0,
            tiled=True,
        ),
        lax.all_to_all(
            value_grad[prompt_total:].astype(jnp.bfloat16)[None],
            "seq",
            split_axis=1,
            concat_axis=0,
            tiled=True,
        ),
    )
    return (
        response_out[None],
        returned[0][home_rank],
        returned[1][home_rank],
        returned[2][home_rank],
        key_summed.astype(jnp.bfloat16),
        value_summed.astype(jnp.bfloat16),
    )


ROW_TILE = 16
LOG2E = 1.4426950408889634
VMEM_BYTES = 64 * 1024 * 1024 - 256 * 1024
MESH = pl.DeviceIdType.MESH


def dot_last(left, right):
    return lax.dot_general(left, right, (((1,), (1,)), ((), ())), preferred_element_type=jnp.float32)


def dot_first(left, right):
    return lax.dot_general(left, right, (((0,), (0,)), ((), ())), preferred_element_type=jnp.float32)


def dot_plain(left, right):
    return lax.dot_general(left, right, (((1,), (0,)), ((), ())), preferred_element_type=jnp.float32)


def wait_bytes(ref, sem):
    pltpu.make_async_copy(ref, ref, sem).wait()


def kernel(
    n, inner, prompt_rows,
    q_hbm, k_hbm, v_hbm, g_hbm, pk_hbm, pv_hbm, len_hbm, home_hbm, seen_hbm,
    out_ref, back_q, dk_hbm, dv_hbm, dpk_hbm, dpv_hbm,
    q_ref, k_ref, v_ref, g_ref, len_ref, home_ref, seen_ref,
    pk_ref, pv_ref, dk_ref, dv_ref, dpk_ref, dpv_ref,
    send_qg, send_kv, send_p, in_qg, in_kv, in_p,
    out_send, grad_q, grad_kv, grad_p, back_kv, back_p, acc,
    sem_load, sem_local, sem_send, sem_kv_out, sem_grad_out,
    sem_p, sem_qg, sem_kv, sem_out, sem_q, sem_grad, sem_gp,
):
    me = lax.axis_index("seq")
    outer = n // inner
    mz, mx = lax.div(me, inner), lax.rem(me, inner)
    rows, width = q_ref.shape[1:]
    kv_width = k_ref.shape[2]
    kv_heads = kv_width // HEAD_DIM
    group = width // kv_width
    total = n * rows
    block = inner * rows
    stacked = group * block
    slot = in_p.shape[0] // n
    scale = 1.0 / HEAD_DIM**0.5

    loads = [
        pltpu.make_async_copy(src, dst, sem_load.at[i])
        for i, (src, dst) in enumerate((
            (len_hbm, len_ref), (home_hbm, home_ref), (seen_hbm, seen_ref),
            (k_hbm, k_ref), (v_hbm, v_ref), (pk_hbm, pk_ref), (pv_hbm, pv_ref),
            (q_hbm, q_ref), (g_hbm, g_ref),
        ))
    ]
    for load in loads:
        load.start()
    in_kv[...] = jnp.zeros_like(in_kv)
    back_kv[...] = jnp.zeros_like(back_kv)
    barrier = pltpu.get_barrier_semaphore()
    for step in range(1, n):
        pl.semaphore_signal(
            barrier, inc=1, device_id={"seq": lax.rem(me + step, n)}, device_id_type=MESH
        )

    def send(src, dst, send_sem, recv_sem, peer):
        pltpu.make_async_remote_copy(
            src_ref=src, dst_ref=dst, send_sem=send_sem, recv_sem=recv_sem,
            device_id={"seq": peer}, device_id_type=MESH,
        ).start()

    def tile(index, size):
        return pl.ds(pl.multiple_of(index * size, size), size)

    def pair_cols(head):
        return head * 2 * HEAD_DIM, head * 2 * HEAD_DIM + HEAD_DIM

    for load in loads[:7]:
        load.wait()
    prompt_pad = jnp.zeros((slot - prompt_rows, HEAD_DIM), jnp.float32)
    for h in range(kv_heads):
        kc, vc = pair_cols(h)
        own = slice(h * HEAD_DIM, (h + 1) * HEAD_DIM)
        for ref, col in ((pk_ref, kc), (pv_ref, vc)):
            part = ref[:, own].astype(jnp.float32)
            if slot > prompt_rows:
                part = jnp.concatenate([part, prompt_pad], axis=0)
            send_p[:, col : col + HEAD_DIM] = part.astype(jnp.bfloat16)

    def resident(rank):
        found = jnp.int32(0)
        for r in range(n):
            found = jnp.where(home_ref[r] == rank, jnp.int32(r), found)
        return found

    sources = [resident(rank) for rank in range(n)]
    for rank in range(n):
        key_rows = k_ref[sources[rank]]
        value_rows = v_ref[sources[rank]]
        for h in range(kv_heads):
            kc, vc = pair_cols(h)
            own = slice(h * HEAD_DIM, (h + 1) * HEAD_DIM)
            send_kv[rank, :, kc : kc + HEAD_DIM] = key_rows[:, own]
            send_kv[rank, :, vc : vc + HEAD_DIM] = value_rows[:, own]
    pl.semaphore_wait(barrier, n - 1)

    partner = mz * inner + (inner - 1 - mx)
    own_rows = tile(me, rows)

    def send_keys(stage):
        for step in range(outer):
            @pl.when(mz + step < outer)
            def _():
                for dx in range(inner):
                    home = stage * inner + dx
                    peer = (mz + step) * inner + dx

                    def go():
                        send(send_kv.at[home], in_kv.at[stage, own_rows, :],
                             sem_kv_out.at[step], sem_kv.at[stage, mz], peer)

                    if step == 0:
                        pl.when(mx != dx)(go)
                    else:
                        go()

    head_width = group * HEAD_DIM

    def send_rows(unit):
        stage, h = unit // kv_heads, unit % kv_heads
        cols = pl.ds(h * head_width, head_width)
        send(send_qg.at[stage * inner + inner - 1 - mx, :, :, cols],
             in_qg.at[stage, :, tile(mx, rows), cols],
             sem_send.at[1], sem_qg.at[unit], partner)

    units = outer * kv_heads
    lead = 4
    send_keys(0)
    for step in range(1, n):
        send(send_p, in_p.at[tile(me, slot), :], sem_send.at[0], sem_p, lax.rem(me + step, n))
    if outer > 1:
        send_keys(1)
    loads[7].wait()
    loads[8].wait()
    for stage in range(outer):
        for dx in range(inner):
            rank = stage * inner + dx
            send_qg[rank, 0] = q_ref[sources[rank]]
            send_qg[rank, 1] = g_ref[sources[rank]]
        for unit in range(stage * kv_heads, (stage + 1) * kv_heads):
            if unit < lead:
                send_rows(unit)
        in_qg[stage, :, tile(mx, rows), :] = send_qg[stage * inner + mx]
        in_kv[stage, own_rows, :] = send_kv[stage * inner + mx]
    in_p[tile(me, slot), :] = send_p[...]

    keys_total = total + n * slot
    position = mz * block + lax.broadcasted_iota(jnp.int32, (block, keys_total), 0)
    col_id = lax.broadcasted_iota(jnp.int32, (block, keys_total), 1)
    in_prompt = col_id - total
    prompt_slot = in_prompt // slot
    prompt_row = in_prompt - prompt_slot * slot
    prompt_id = prompt_slot * prompt_rows + prompt_row
    far = jnp.int32(2**30)
    prompt_rank = jnp.where(prompt_row < prompt_rows, prompt_id, far)
    ahead = col_id - position
    live_position = mz * block + lax.broadcasted_iota(jnp.int32, (block, HEAD_DIM), 0)

    def per_head(rows_of_heads, factor, combine):
        shape = rows_of_heads.shape
        return combine(rows_of_heads.reshape(group, block, shape[1]), factor[None]).reshape(shape)

    wait_bytes(in_p.at[0 : (n - 1) * slot, :], sem_p)
    acc[...] = jnp.zeros_like(acc)
    for stage in range(outer):
        home = stage * inner + mx
        source = resident(home)
        length = len_ref[source]
        visible = seen_ref[source]
        allowed = jnp.where(col_id < total, ahead, prompt_rank - visible + 1) <= 0
        bias = jnp.where(allowed, 0.0, NEG_FILL)
        live = (live_position < length).astype(jnp.float32)
        for step in range(outer):
            @pl.when(step < mz)
            def _():
                wait_bytes(in_kv.at[stage, 0:block, :], sem_kv.at[stage, step])

            @pl.when(step == mz)
            def _():
                wait_bytes(in_kv.at[stage, 0:rows, :], sem_kv.at[stage, step])
        if stage + 2 < outer:
            send_keys(stage + 2)
        for h in range(kv_heads):
            unit = stage * kv_heads + h
            cols = pl.ds(h * head_width, head_width)
            wait_bytes(in_qg.at[stage, :, 0:rows, cols], sem_qg.at[unit])
            if unit + lead < units:
                send_rows(unit + lead)
            kc, vc = pair_cols(h)
            keys = jnp.concatenate(
                [in_kv[stage, :, kc : kc + HEAD_DIM], in_p[:, kc : kc + HEAD_DIM]], axis=0
            )
            values = jnp.concatenate(
                [in_kv[stage, :, vc : vc + HEAD_DIM], in_p[:, vc : vc + HEAD_DIM]], axis=0
            )
            heads = [
                slice((h * group + a) * HEAD_DIM, (h * group + a + 1) * HEAD_DIM)
                for a in range(group)
            ]
            query = jnp.concatenate([in_qg[stage, 0, :, c] for c in heads], axis=0)
            grad = jnp.concatenate([in_qg[stage, 1, :, c] for c in heads], axis=0)
            grad_wide = per_head(grad.astype(jnp.float32), live, jnp.multiply)
            grad = grad_wide.astype(jnp.bfloat16)
            logits = per_head(dot_last(query, keys) * (scale * LOG2E), bias, jnp.add)
            exped = jnp.exp2(logits - jnp.max(logits, axis=1, keepdims=True))
            prob = exped * (1.0 / jnp.sum(exped, axis=1, keepdims=True))
            weights = prob.astype(jnp.bfloat16)
            output = per_head(dot_plain(weights, values), live, jnp.multiply).astype(jnp.bfloat16)
            row_dot = jnp.sum(grad_wide * output.astype(jnp.float32), axis=1, keepdims=True)
            dlogit = (prob * (dot_last(grad, values) - row_dot)).astype(jnp.bfloat16)
            dquery = (dot_plain(dlogit, keys) * scale).astype(jnp.bfloat16)
            for a in range(group):
                part = slice(a * block, (a + 1) * block)
                out_send[stage, :, heads[a]] = output[part]
                grad_q[stage, :, heads[a]] = dquery[part]
            dkey = dot_first(dlogit, query) * scale
            dvalue = dot_first(weights, grad)
            for col, part in ((kc, dkey), (vc, dvalue)):
                grad_kv[stage, :, col : col + HEAD_DIM] = part[:total].astype(jnp.bfloat16)
                acc[:, col : col + HEAD_DIM] += part[total:]

            @pl.when(mz != stage)
            def _():
                send(out_send.at[stage, :, cols], out_ref.at[0, tile(mz, block), cols],
                     sem_send.at[2], sem_out, home)

            @pl.when(mz == stage)
            def _():
                pltpu.make_async_copy(
                    out_send.at[stage, :, cols], out_ref.at[0, tile(mz, block), cols], sem_local.at[0]
                ).start()

            send(grad_q.at[stage, tile(inner - 1 - mx, rows), cols], back_q.at[home, :, cols],
                 sem_send.at[3], sem_q, partner)
            pltpu.make_async_copy(
                grad_q.at[stage, tile(mx, rows), cols], back_q.at[home, :, cols], sem_local.at[1]
            ).start()

        for step in range(outer):
            @pl.when(mz - step >= 0)
            def _():
                for dx in range(inner):
                    chunk = (mz - step) * inner + dx

                    def go():
                        send(grad_kv.at[stage, tile(chunk, rows), :], back_kv.at[mz, home],
                             sem_grad_out.at[step], sem_grad.at[mz], chunk)

                    if step == 0:
                        pl.when(mx != dx)(go)
                    else:
                        go()
        back_kv[mz, home] = grad_kv[stage, own_rows, :]
    grad_p[...] = acc[...].astype(jnp.bfloat16)
    for step in range(1, n):
        peer = lax.rem(me + step, n)
        send(grad_p.at[tile(peer, slot), :], back_p.at[me], sem_send.at[4], sem_gp, peer)
    back_p[me] = grad_p[tile(me, slot), :]

    for step in range(outer):
        @pl.when(step > mz)
        def _():
            wait_bytes(back_kv.at[step], sem_grad.at[step])

        @pl.when(step == mz)
        def _():
            wait_bytes(back_kv.at[step, 0:outer], sem_grad.at[step])
    for r in range(n):
        home = home_ref[r]
        summed = back_kv[0, home].astype(jnp.float32)
        for step in range(1, outer):
            summed = summed + back_kv[step, home].astype(jnp.float32)
        summed = summed.astype(jnp.bfloat16)
        for h in range(kv_heads):
            kc, vc = pair_cols(h)
            own = slice(h * HEAD_DIM, (h + 1) * HEAD_DIM)
            dk_ref[r, :, own] = summed[:, kc : kc + HEAD_DIM]
            dv_ref[r, :, own] = summed[:, vc : vc + HEAD_DIM]
    wait_bytes(back_p.at[0 : n - 1], sem_gp)
    prompt_sum = back_p[0].astype(jnp.float32)
    for rank in range(1, n):
        prompt_sum = prompt_sum + back_p[rank].astype(jnp.float32)
    for h in range(kv_heads):
        kc, vc = pair_cols(h)
        own = slice(h * HEAD_DIM, (h + 1) * HEAD_DIM)
        dpk_ref[:, own] = prompt_sum[:prompt_rows, kc : kc + HEAD_DIM].astype(jnp.bfloat16)
        dpv_ref[:, own] = prompt_sum[:prompt_rows, vc : vc + HEAD_DIM].astype(jnp.bfloat16)

    stores = [
        pltpu.make_async_copy(src, dst, sem_load.at[i])
        for i, (src, dst) in enumerate((
            (dk_ref, dk_hbm), (dv_ref, dv_hbm), (dpk_ref, dpk_hbm), (dpv_ref, dpv_hbm),
        ))
    ]
    for store in stores:
        store.start()
    wait_bytes(out_send.at[0], sem_local.at[0])
    wait_bytes(back_q.at[0:outer], sem_local.at[1])
    wait_bytes(out_send.at[0 : outer - 1], sem_out)
    wait_bytes(back_q.at[0:outer], sem_q)
    wait_bytes(back_p.at[0 : n - 1], sem_send.at[0])
    wait_bytes(in_qg.at[:, :, 0:rows, :], sem_send.at[1])
    wait_bytes(out_send.at[0 : outer - 1], sem_send.at[2])
    wait_bytes(back_q.at[0:outer], sem_send.at[3])
    wait_bytes(back_p.at[0 : n - 1], sem_send.at[4])
    for sem in (sem_kv_out, sem_grad_out):
        for step in range(outer):
            reached = mz + step < outer if sem is sem_kv_out else mz - step >= 0

            @pl.when(reached)
            def _():
                wait_bytes(send_kv.at[0 : outer if step == 0 else n], sem.at[step])
    for store in stores:
        store.wait()


def place_kernel(n, *refs):
    sources, home_hbm = refs[:6], refs[6]
    results, held, home_ref = refs[7:13], refs[13:19], refs[19]
    sem_in, sem_out, sem_row, sem_home = refs[20:]
    ranks = pltpu.make_async_copy(home_hbm, home_ref, sem_home)
    ranks.start()
    reads = [
        pltpu.make_async_copy(src, dst, sem_in.at[i]) for i, (src, dst) in enumerate(zip(sources, held))
    ]
    for copy in reads:
        copy.start()
    writes = []
    for i in (0, 2, 3, 4, 5):
        reads[i].wait()
        writes.append(pltpu.make_async_copy(held[i], results[i], sem_out.at[i]))
        writes[-1].start()
    reads[1].wait()
    ranks.wait()
    for r in range(n):
        writes.append(pltpu.make_async_copy(held[1].at[home_ref[r]], results[1].at[r], sem_row.at[r]))
        writes[-1].start()
    for copy in writes:
        copy.wait()


def kernel_body(*arrays):
    query, key, _, _, prompt_key, _, lengths, home_rank, _ = arrays
    n = lax.axis_size("seq")
    inner = 2
    outer = n // inner
    rows, width = query.shape[1:]
    kv_width = key.shape[2]
    prompt_rows = prompt_key.shape[0]
    slot = -(-prompt_rows // ROW_TILE) * ROW_TILE
    total = n * rows
    bf16 = jnp.bfloat16
    hbm = pl.BlockSpec(memory_space=pltpu.HBM)
    shapes = (
        jax.ShapeDtypeStruct((1, total, width), bf16),
        jax.ShapeDtypeStruct(query.shape, bf16),
        jax.ShapeDtypeStruct(key.shape, bf16),
        jax.ShapeDtypeStruct(key.shape, bf16),
        jax.ShapeDtypeStruct(prompt_key.shape, bf16),
        jax.ShapeDtypeStruct(prompt_key.shape, bf16),
    )
    dma = pltpu.SemaphoreType.DMA
    results = pl.pallas_call(
        functools.partial(kernel, n, inner, prompt_rows),
        out_shape=shapes,
        in_specs=[hbm] * 9,
        out_specs=(hbm,) * 6,
        scratch_shapes=[
            pltpu.VMEM(query.shape, bf16),
            pltpu.VMEM(key.shape, bf16),
            pltpu.VMEM(key.shape, bf16),
            pltpu.VMEM(query.shape, bf16),
            pltpu.SMEM(lengths.shape, jnp.int32),
            pltpu.SMEM(lengths.shape, jnp.int32),
            pltpu.SMEM(lengths.shape, jnp.int32),
            pltpu.VMEM(prompt_key.shape, bf16),
            pltpu.VMEM(prompt_key.shape, bf16),
            *(pltpu.VMEM(shape.shape, bf16) for shape in shapes[2:]),
            pltpu.VMEM((n, 2, rows, width), bf16),
            pltpu.VMEM((n, rows, 2 * kv_width), bf16),
            pltpu.VMEM((slot, 2 * kv_width), bf16),
            pltpu.VMEM((outer, 2, inner * rows, width), bf16),
            pltpu.VMEM((outer, total, 2 * kv_width), bf16),
            pltpu.VMEM((n * slot, 2 * kv_width), bf16),
            pltpu.VMEM((outer, inner * rows, width), bf16),
            pltpu.VMEM((outer, inner * rows, width), bf16),
            pltpu.VMEM((outer, total, 2 * kv_width), bf16),
            pltpu.VMEM((n * slot, 2 * kv_width), bf16),
            pltpu.VMEM((outer, n, rows, 2 * kv_width), bf16),
            pltpu.VMEM((n, slot, 2 * kv_width), bf16),
            pltpu.VMEM((n * slot, 2 * kv_width), jnp.float32),
            dma((9,)), dma((2,)), dma((5,)), dma((outer,)), dma((outer,)),
            dma, dma((outer * (kv_width // HEAD_DIM),)), dma((outer, outer)), dma, dma, dma((outer,)), dma,
        ],
        compiler_params=pltpu.CompilerParams(
            collective_id=0, has_side_effects=True, vmem_limit_bytes=VMEM_BYTES
        ),
    )(*arrays)
    return pl.pallas_call(
        functools.partial(place_kernel, n),
        out_shape=shapes,
        in_specs=[hbm] * 7,
        out_specs=(hbm,) * 6,
        scratch_shapes=[
            *(pltpu.VMEM(shape.shape, bf16) for shape in shapes),
            pltpu.SMEM(home_rank.shape, jnp.int32),
            dma((6,)), dma((6,)), dma((n,)), dma,
        ],
        compiler_params=pltpu.CompilerParams(vmem_limit_bytes=VMEM_BYTES),
    )(*results, home_rank)


def body(*arrays):
    rows = arrays[0].shape[1]
    slot = -(-arrays[4].shape[0] // ROW_TILE) * ROW_TILE
    if rows % ROW_TILE == 0 and slot == rows and lax.axis_size("seq") % 2 == 0:
        return kernel_body(*arrays)
    return collective_body(*arrays)


def solution(mesh):
    placed = (
        P("group", "seq", "head"),
        P("group", "seq", "head"),
        P("group", "seq", "head"),
        P("group", "seq", "head"),
        P(("group", "seq"), "head"),
        P(("group", "seq"), "head"),
        P("group"),
        P("group"),
        P("group"),
    )
    return jax.shard_map(
        body,
        mesh=mesh,
        in_specs=placed,
        out_specs=(
            P(("group", "seq"), None, "head"),
            P("group", "seq", "head"),
            P("group", "seq", "head"),
            P("group", "seq", "head"),
            P(("group", "seq"), "head"),
            P(("group", "seq"), "head"),
        ),
        check_vma=False,
    )
```

```python
import functools

import jax
import jax.numpy as jnp
from jax import lax
from jax.experimental import pallas as pl
from jax.experimental.pallas import tpu as pltpu
from jax.sharding import PartitionSpec as P

HEAD_DIM = 128


NEG_FILL = -1e30


def head_logits(queries, all_keys, allowed, head_index, group_size, scale_factor):
    row_count = queries.shape[0]
    low = head_index * group_size * HEAD_DIM
    high = (head_index + 1) * group_size * HEAD_DIM
    query_head = queries[:, low:high].reshape(row_count, group_size, HEAD_DIM)
    key_head = all_keys[:, head_index * HEAD_DIM : (head_index + 1) * HEAD_DIM]
    logits = (
        jnp.einsum("rhd,kd->rhk", query_head, key_head, preferred_element_type=jnp.float32)
        * scale_factor
    )
    return (query_head, key_head, jnp.where(allowed[:, None, :], logits, NEG_FILL))


def forward(queries, all_keys, all_values, allowed, live_rows, scale_factor):
    row_count = queries.shape[0]
    kv_count = all_keys.shape[1] // HEAD_DIM
    group_size = queries.shape[1] // all_keys.shape[1]
    outputs = []
    totals = []
    for head_index in range(kv_count):
        query_head, key_head, logits = head_logits(
            queries, all_keys, allowed, head_index, group_size, scale_factor
        )
        value_head = all_values[:, head_index * HEAD_DIM : (head_index + 1) * HEAD_DIM]
        row_max = jnp.max(logits, axis=2, keepdims=True)
        log_total = row_max + jnp.log(jnp.sum(jnp.exp(logits - row_max), axis=2, keepdims=True))
        weights = jnp.exp(logits - log_total).astype(jnp.bfloat16)
        mixed = jnp.einsum("rhk,kd->rhd", weights, value_head, preferred_element_type=jnp.float32)
        output_head = jnp.where(live_rows[:, None, None], mixed, 0.0).astype(jnp.bfloat16)
        outputs.append(output_head.reshape(row_count, group_size * HEAD_DIM))
        totals.append(log_total)
    return (jnp.concatenate(outputs, axis=1), totals)


def head_terms(grad_rows, live_rows, output, head_index, group_size):
    row_count = grad_rows.shape[0]
    low = head_index * group_size * HEAD_DIM
    high = (head_index + 1) * group_size * HEAD_DIM
    grad_head = jnp.where(live_rows[:, None], grad_rows[:, low:high], jnp.zeros((), jnp.bfloat16))
    grad_head = grad_head.reshape(row_count, group_size, HEAD_DIM)
    output_head = lax.optimization_barrier(output[:, low:high]).reshape(
        row_count, group_size, HEAD_DIM
    )
    row_dot = jnp.sum(
        grad_head.astype(jnp.float32) * output_head.astype(jnp.float32), axis=2, keepdims=True
    )
    return (grad_head, row_dot)


def backward(
    queries, all_keys, all_values, grad_rows, allowed, live_rows, output, totals, scale_factor
):
    row_count = queries.shape[0]
    kv_count = all_keys.shape[1] // HEAD_DIM
    group_size = queries.shape[1] // all_keys.shape[1]
    query_grads = []
    key_grads = []
    value_grads = []
    for head_index in range(kv_count):
        query_head, key_head, logits = head_logits(
            queries, all_keys, allowed, head_index, group_size, scale_factor
        )
        value_head = all_values[:, head_index * HEAD_DIM : (head_index + 1) * HEAD_DIM]
        prob = jnp.exp(logits - totals[head_index])
        weights = prob.astype(jnp.bfloat16)
        grad_head, row_dot = head_terms(grad_rows, live_rows, output, head_index, group_size)
        spread = jnp.einsum(
            "rhd,kd->rhk", grad_head, value_head, preferred_element_type=jnp.float32
        )
        dlogit = (prob * (spread - row_dot)).astype(jnp.bfloat16)
        query_part = (
            jnp.einsum("rhk,kd->rhd", dlogit, key_head, preferred_element_type=jnp.float32)
            * scale_factor
        )
        query_grads.append(query_part.reshape(row_count, group_size * HEAD_DIM))
        key_grads.append(
            jnp.einsum("rhk,rhd->kd", dlogit, query_head, preferred_element_type=jnp.float32)
            * scale_factor
        )
        value_grads.append(
            jnp.einsum("rhk,rhd->kd", weights, grad_head, preferred_element_type=jnp.float32)
        )
    return (
        jnp.concatenate(query_grads, axis=1),
        jnp.concatenate(key_grads, axis=1),
        jnp.concatenate(value_grads, axis=1),
    )


def collective_body(
    response_query,
    response_key,
    response_value,
    response_grad,
    prompt_key,
    prompt_value,
    lengths,
    home_rank,
    prompt_seen,
):
    rank_count = home_rank.shape[0]
    rank_ids = jnp.arange(rank_count, dtype=jnp.int32)
    resident = jnp.sum(
        jnp.where(home_rank[None, :] == rank_ids[:, None], rank_ids[None, :], 0), axis=1
    )
    own_rank = lax.axis_index("seq")
    scale_factor = 1.0 / HEAD_DIM**0.5
    arrived = (
        lax.all_to_all(response_query[resident], "seq", split_axis=0, concat_axis=1, tiled=True),
        lax.all_to_all(response_key[resident], "seq", split_axis=0, concat_axis=1, tiled=True),
        lax.all_to_all(response_value[resident], "seq", split_axis=0, concat_axis=1, tiled=True),
        lax.all_to_all(response_grad[resident], "seq", split_axis=0, concat_axis=1, tiled=True),
    )
    queries = arrived[0][0]
    own_keys = arrived[1][0]
    own_values = arrived[2][0]
    grad_rows = arrived[3][0]
    own_response = resident[own_rank]
    length = lengths[own_response]
    visible = prompt_seen[own_response]
    max_length = queries.shape[0]
    prompt_rows = prompt_key.shape[0]
    prompt_total = prompt_rows * lax.axis_size("seq")
    positions = jnp.arange(max_length, dtype=jnp.int32)
    prompt_cols = jnp.arange(prompt_total, dtype=jnp.int32)
    seen_part = jnp.broadcast_to(prompt_cols[None, :] < visible, (max_length, prompt_total))
    allowed = jnp.concatenate([seen_part, positions[None, :] <= positions[:, None]], axis=1)
    live_rows = positions < length
    gathered_keys, gathered_values = (
        lax.all_gather(prompt_key, "seq", axis=0, tiled=True),
        lax.all_gather(prompt_value, "seq", axis=0, tiled=True),
    )
    all_keys = jnp.concatenate([gathered_keys, own_keys], axis=0)
    all_values = jnp.concatenate([gathered_values, own_values], axis=0)
    response_out, response_totals = forward(
        queries, all_keys, all_values, allowed, live_rows, scale_factor
    )
    query_grad, key_grad, value_grad = backward(
        queries,
        all_keys,
        all_values,
        grad_rows,
        allowed,
        live_rows,
        response_out,
        response_totals,
        scale_factor,
    )
    key_summed, value_summed = (
        lax.psum_scatter(key_grad[:prompt_total], "seq", scatter_dimension=0, tiled=True),
        lax.psum_scatter(value_grad[:prompt_total], "seq", scatter_dimension=0, tiled=True),
    )
    returned = (
        lax.all_to_all(
            query_grad.astype(jnp.bfloat16)[None], "seq", split_axis=1, concat_axis=0, tiled=True
        ),
        lax.all_to_all(
            key_grad[prompt_total:].astype(jnp.bfloat16)[None],
            "seq",
            split_axis=1,
            concat_axis=0,
            tiled=True,
        ),
        lax.all_to_all(
            value_grad[prompt_total:].astype(jnp.bfloat16)[None],
            "seq",
            split_axis=1,
            concat_axis=0,
            tiled=True,
        ),
    )
    return (
        response_out[None],
        returned[0][home_rank],
        returned[1][home_rank],
        returned[2][home_rank],
        key_summed.astype(jnp.bfloat16),
        value_summed.astype(jnp.bfloat16),
    )


ROW_TILE = 16
LOG2E = 1.4426950408889634
VMEM_BYTES = 64 * 1024 * 1024 - 256 * 1024
MESH = pl.DeviceIdType.MESH


def dot_last(left, right):
    return lax.dot_general(left, right, (((1,), (1,)), ((), ())), preferred_element_type=jnp.float32)


def dot_first(left, right):
    return lax.dot_general(left, right, (((0,), (0,)), ((), ())), preferred_element_type=jnp.float32)


def dot_plain(left, right):
    return lax.dot_general(left, right, (((1,), (0,)), ((), ())), preferred_element_type=jnp.float32)


def wait_bytes(ref, sem):
    pltpu.make_async_copy(ref, ref, sem).wait()


def kernel(
    n, inner, prompt_rows,
    q_hbm, k_hbm, v_hbm, g_hbm, pk_hbm, pv_hbm, len_hbm, home_hbm, seen_hbm,
    out_ref, back_q, dk_hbm, dv_hbm, dpk_hbm, dpv_hbm,
    q_ref, k_ref, v_ref, g_ref, len_ref, home_ref, seen_ref,
    pk_ref, pv_ref, dk_ref, dv_ref, dpk_ref, dpv_ref,
    send_qg, send_kv, send_p, in_qg, in_kv, in_p,
    out_send, grad_q, grad_kv, grad_p, back_kv, back_p, acc,
    sem_load, sem_local, sem_send, sem_kv_out, sem_grad_out,
    sem_p, sem_qg, sem_kv, sem_out, sem_q, sem_grad, sem_gp,
):
    me = lax.axis_index("seq")
    outer = n // inner
    mz, mx = lax.div(me, inner), lax.rem(me, inner)
    rows, width = q_ref.shape[1:]
    kv_width = k_ref.shape[2]
    kv_heads = kv_width // HEAD_DIM
    group = width // kv_width
    total = n * rows
    block = inner * rows
    stacked = group * block
    slot = in_p.shape[0] // n
    scale = 1.0 / HEAD_DIM**0.5

    loads = [
        pltpu.make_async_copy(src, dst, sem_load.at[i])
        for i, (src, dst) in enumerate((
            (len_hbm, len_ref), (home_hbm, home_ref), (seen_hbm, seen_ref),
            (k_hbm, k_ref), (v_hbm, v_ref), (pk_hbm, pk_ref), (pv_hbm, pv_ref),
            (q_hbm, q_ref), (g_hbm, g_ref),
        ))
    ]
    for load in loads:
        load.start()
    in_kv[...] = jnp.zeros_like(in_kv)
    back_kv[...] = jnp.zeros_like(back_kv)
    barrier = pltpu.get_barrier_semaphore()
    for step in range(1, n):
        pl.semaphore_signal(
            barrier, inc=1, device_id={"seq": lax.rem(me + step, n)}, device_id_type=MESH
        )

    def send(src, dst, send_sem, recv_sem, peer):
        pltpu.make_async_remote_copy(
            src_ref=src, dst_ref=dst, send_sem=send_sem, recv_sem=recv_sem,
            device_id={"seq": peer}, device_id_type=MESH,
        ).start()

    def tile(index, size):
        return pl.ds(pl.multiple_of(index * size, size), size)

    def pair_cols(head):
        return head * 2 * HEAD_DIM, head * 2 * HEAD_DIM + HEAD_DIM

    for load in loads[:7]:
        load.wait()
    prompt_pad = jnp.zeros((slot - prompt_rows, HEAD_DIM), jnp.float32)
    for h in range(kv_heads):
        kc, vc = pair_cols(h)
        own = slice(h * HEAD_DIM, (h + 1) * HEAD_DIM)
        for ref, col in ((pk_ref, kc), (pv_ref, vc)):
            part = ref[:, own].astype(jnp.float32)
            if slot > prompt_rows:
                part = jnp.concatenate([part, prompt_pad], axis=0)
            send_p[:, col : col + HEAD_DIM] = part.astype(jnp.bfloat16)

    def resident(rank):
        found = jnp.int32(0)
        for r in range(n):
            found = jnp.where(home_ref[r] == rank, jnp.int32(r), found)
        return found

    sources = [resident(rank) for rank in range(n)]
    for rank in range(n):
        key_rows = k_ref[sources[rank]]
        value_rows = v_ref[sources[rank]]
        for h in range(kv_heads):
            kc, vc = pair_cols(h)
            own = slice(h * HEAD_DIM, (h + 1) * HEAD_DIM)
            send_kv[rank, :, kc : kc + HEAD_DIM] = key_rows[:, own]
            send_kv[rank, :, vc : vc + HEAD_DIM] = value_rows[:, own]
    pl.semaphore_wait(barrier, n - 1)

    partner = mz * inner + (inner - 1 - mx)
    own_rows = tile(me, rows)

    def send_keys(stage):
        for step in range(outer):
            @pl.when(mz + step < outer)
            def _():
                for dx in range(inner):
                    home = stage * inner + dx
                    peer = (mz + step) * inner + dx

                    def go():
                        send(send_kv.at[home], in_kv.at[stage, own_rows, :],
                             sem_kv_out.at[step], sem_kv.at[stage, mz], peer)

                    if step == 0:
                        pl.when(mx != dx)(go)
                    else:
                        go()

    head_width = group * HEAD_DIM

    def send_rows(unit):
        stage, h = unit // kv_heads, unit % kv_heads
        cols = pl.ds(h * head_width, head_width)
        send(send_qg.at[stage * inner + inner - 1 - mx, :, :, cols],
             in_qg.at[stage, :, tile(mx, rows), cols],
             sem_send.at[1], sem_qg.at[unit], partner)

    units = outer * kv_heads
    lead = 4
    send_keys(0)
    for step in range(1, n):
        send(send_p, in_p.at[tile(me, slot), :], sem_send.at[0], sem_p, lax.rem(me + step, n))
    if outer > 1:
        send_keys(1)
    loads[7].wait()
    loads[8].wait()
    for stage in range(outer):
        for dx in range(inner):
            rank = stage * inner + dx
            send_qg[rank, 0] = q_ref[sources[rank]]
            send_qg[rank, 1] = g_ref[sources[rank]]
        for unit in range(stage * kv_heads, (stage + 1) * kv_heads):
            if unit < lead:
                send_rows(unit)
        in_qg[stage, :, tile(mx, rows), :] = send_qg[stage * inner + mx]
        in_kv[stage, own_rows, :] = send_kv[stage * inner + mx]
    in_p[tile(me, slot), :] = send_p[...]

    keys_total = total + n * slot
    position = mz * block + lax.broadcasted_iota(jnp.int32, (block, keys_total), 0)
    col_id = lax.broadcasted_iota(jnp.int32, (block, keys_total), 1)
    in_prompt = col_id - total
    prompt_slot = in_prompt // slot
    prompt_row = in_prompt - prompt_slot * slot
    prompt_id = prompt_slot * prompt_rows + prompt_row
    far = jnp.int32(2**30)
    prompt_rank = jnp.where(prompt_row < prompt_rows, prompt_id, far)
    ahead = col_id - position
    live_position = mz * block + lax.broadcasted_iota(jnp.int32, (block, HEAD_DIM), 0)

    def per_head(rows_of_heads, factor, combine):
        shape = rows_of_heads.shape
        return combine(rows_of_heads.reshape(group, block, shape[1]), factor[None]).reshape(shape)

    wait_bytes(in_p.at[0 : (n - 1) * slot, :], sem_p)
    acc[...] = jnp.zeros_like(acc)
    for stage in range(outer):
        home = stage * inner + mx
        source = resident(home)
        length = len_ref[source]
        visible = seen_ref[source]
        allowed = jnp.where(col_id < total, ahead, prompt_rank - visible + 1) <= 0
        bias = jnp.where(allowed, 0.0, NEG_FILL)
        live = (live_position < length).astype(jnp.float32)
        for step in range(outer):
            @pl.when(step < mz)
            def _():
                wait_bytes(in_kv.at[stage, 0:block, :], sem_kv.at[stage, step])

            @pl.when(step == mz)
            def _():
                wait_bytes(in_kv.at[stage, 0:rows, :], sem_kv.at[stage, step])
        if stage + 2 < outer:
            send_keys(stage + 2)
        for h in range(kv_heads):
            unit = stage * kv_heads + h
            cols = pl.ds(h * head_width, head_width)
            wait_bytes(in_qg.at[stage, :, 0:rows, cols], sem_qg.at[unit])
            if unit + lead < units:
                send_rows(unit + lead)
            kc, vc = pair_cols(h)
            keys = jnp.concatenate(
                [in_kv[stage, :, kc : kc + HEAD_DIM], in_p[:, kc : kc + HEAD_DIM]], axis=0
            )
            values = jnp.concatenate(
                [in_kv[stage, :, vc : vc + HEAD_DIM], in_p[:, vc : vc + HEAD_DIM]], axis=0
            )
            heads = [
                slice((h * group + a) * HEAD_DIM, (h * group + a + 1) * HEAD_DIM)
                for a in range(group)
            ]
            query = jnp.concatenate([in_qg[stage, 0, :, c] for c in heads], axis=0)
            grad = jnp.concatenate([in_qg[stage, 1, :, c] for c in heads], axis=0)
            grad_wide = per_head(grad.astype(jnp.float32), live, jnp.multiply)
            grad = grad_wide.astype(jnp.bfloat16)
            logits = per_head(dot_last(query, keys) * (scale * LOG2E), bias, jnp.add)
            exped = jnp.exp2(logits - jnp.max(logits, axis=1, keepdims=True))
            prob = exped * (1.0 / jnp.sum(exped, axis=1, keepdims=True))
            weights = prob.astype(jnp.bfloat16)
            output = per_head(dot_plain(weights, values), live, jnp.multiply).astype(jnp.bfloat16)
            row_dot = jnp.sum(grad_wide * output.astype(jnp.float32), axis=1, keepdims=True)
            dlogit = (prob * (dot_last(grad, values) - row_dot)).astype(jnp.bfloat16)
            dquery = (dot_plain(dlogit, keys) * scale).astype(jnp.bfloat16)
            for a in range(group):
                part = slice(a * block, (a + 1) * block)
                out_send[stage, :, heads[a]] = output[part]
                grad_q[stage, :, heads[a]] = dquery[part]
            dkey = dot_first(dlogit, query) * scale
            dvalue = dot_first(weights, grad)
            for col, part in ((kc, dkey), (vc, dvalue)):
                grad_kv[stage, :, col : col + HEAD_DIM] = part[:total].astype(jnp.bfloat16)
                acc[:, col : col + HEAD_DIM] += part[total:]

            if h == kv_heads - 1:
                for step in range(outer):
                    @pl.when(mz - step >= 0)
                    def _():
                        for dx in range(inner):
                            chunk = (mz - step) * inner + dx

                            def go():
                                send(grad_kv.at[stage, tile(chunk, rows), :], back_kv.at[mz, home],
                                     sem_grad_out.at[step], sem_grad.at[mz], chunk)

                            if step == 0:
                                pl.when(mx != dx)(go)
                            else:
                                go()
            if unit == units - 1:
                grad_p[...] = acc[...].astype(jnp.bfloat16)
                for step in range(1, n):
                    peer = lax.rem(me + step, n)
                    send(grad_p.at[tile(peer, slot), :], back_p.at[me], sem_send.at[4], sem_gp, peer)

            @pl.when(mz != stage)
            def _():
                send(out_send.at[stage, :, cols], out_ref.at[0, tile(mz, block), cols],
                     sem_send.at[2], sem_out, home)

            @pl.when(mz == stage)
            def _():
                pltpu.make_async_copy(
                    out_send.at[stage, :, cols], out_ref.at[0, tile(mz, block), cols], sem_local.at[0]
                ).start()

            send(grad_q.at[stage, tile(inner - 1 - mx, rows), cols], back_q.at[home, :, cols],
                 sem_send.at[3], sem_q, partner)
            pltpu.make_async_copy(
                grad_q.at[stage, tile(mx, rows), cols], back_q.at[home, :, cols], sem_local.at[1]
            ).start()

        back_kv[mz, home] = grad_kv[stage, own_rows, :]
    back_p[me] = grad_p[tile(me, slot), :]

    for step in range(outer):
        @pl.when(step > mz)
        def _():
            wait_bytes(back_kv.at[step], sem_grad.at[step])

        @pl.when(step == mz)
        def _():
            wait_bytes(back_kv.at[step, 0:outer], sem_grad.at[step])
    for r in range(n):
        home = home_ref[r]
        summed = back_kv[0, home].astype(jnp.float32)
        for step in range(1, outer):
            summed = summed + back_kv[step, home].astype(jnp.float32)
        summed = summed.astype(jnp.bfloat16)
        for h in range(kv_heads):
            kc, vc = pair_cols(h)
            own = slice(h * HEAD_DIM, (h + 1) * HEAD_DIM)
            dk_ref[r, :, own] = summed[:, kc : kc + HEAD_DIM]
            dv_ref[r, :, own] = summed[:, vc : vc + HEAD_DIM]
    wait_bytes(back_p.at[0 : n - 1], sem_gp)
    prompt_sum = back_p[0].astype(jnp.float32)
    for rank in range(1, n):
        prompt_sum = prompt_sum + back_p[rank].astype(jnp.float32)
    for h in range(kv_heads):
        kc, vc = pair_cols(h)
        own = slice(h * HEAD_DIM, (h + 1) * HEAD_DIM)
        dpk_ref[:, own] = prompt_sum[:prompt_rows, kc : kc + HEAD_DIM].astype(jnp.bfloat16)
        dpv_ref[:, own] = prompt_sum[:prompt_rows, vc : vc + HEAD_DIM].astype(jnp.bfloat16)

    stores = [
        pltpu.make_async_copy(src, dst, sem_load.at[i])
        for i, (src, dst) in enumerate((
            (dk_ref, dk_hbm), (dv_ref, dv_hbm), (dpk_ref, dpk_hbm), (dpv_ref, dpv_hbm),
        ))
    ]
    for store in stores:
        store.start()
    wait_bytes(out_send.at[0], sem_local.at[0])
    wait_bytes(back_q.at[0:outer], sem_local.at[1])
    wait_bytes(out_send.at[0 : outer - 1], sem_out)
    wait_bytes(back_q.at[0:outer], sem_q)
    wait_bytes(back_p.at[0 : n - 1], sem_send.at[0])
    wait_bytes(in_qg.at[:, :, 0:rows, :], sem_send.at[1])
    wait_bytes(out_send.at[0 : outer - 1], sem_send.at[2])
    wait_bytes(back_q.at[0:outer], sem_send.at[3])
    wait_bytes(back_p.at[0 : n - 1], sem_send.at[4])
    for sem in (sem_kv_out, sem_grad_out):
        for step in range(outer):
            reached = mz + step < outer if sem is sem_kv_out else mz - step >= 0

            @pl.when(reached)
            def _():
                wait_bytes(send_kv.at[0 : outer if step == 0 else n], sem.at[step])
    for store in stores:
        store.wait()


def place_kernel(n, *refs):
    sources, home_hbm = refs[:6], refs[6]
    results, held, home_ref = refs[7:13], refs[13:19], refs[19]
    sem_in, sem_out, sem_row, sem_home = refs[20:]
    ranks = pltpu.make_async_copy(home_hbm, home_ref, sem_home)
    ranks.start()
    reads = [
        pltpu.make_async_copy(src, dst, sem_in.at[i]) for i, (src, dst) in enumerate(zip(sources, held))
    ]
    for copy in reads:
        copy.start()
    writes = []
    for i in (0, 2, 3, 4, 5):
        reads[i].wait()
        writes.append(pltpu.make_async_copy(held[i], results[i], sem_out.at[i]))
        writes[-1].start()
    reads[1].wait()
    ranks.wait()
    for r in range(n):
        writes.append(pltpu.make_async_copy(held[1].at[home_ref[r]], results[1].at[r], sem_row.at[r]))
        writes[-1].start()
    for copy in writes:
        copy.wait()


def kernel_body(*arrays):
    query, key, _, _, prompt_key, _, lengths, home_rank, _ = arrays
    n = lax.axis_size("seq")
    inner = 2
    outer = n // inner
    rows, width = query.shape[1:]
    kv_width = key.shape[2]
    prompt_rows = prompt_key.shape[0]
    slot = -(-prompt_rows // ROW_TILE) * ROW_TILE
    total = n * rows
    bf16 = jnp.bfloat16
    hbm = pl.BlockSpec(memory_space=pltpu.HBM)
    shapes = (
        jax.ShapeDtypeStruct((1, total, width), bf16),
        jax.ShapeDtypeStruct(query.shape, bf16),
        jax.ShapeDtypeStruct(key.shape, bf16),
        jax.ShapeDtypeStruct(key.shape, bf16),
        jax.ShapeDtypeStruct(prompt_key.shape, bf16),
        jax.ShapeDtypeStruct(prompt_key.shape, bf16),
    )
    dma = pltpu.SemaphoreType.DMA
    results = pl.pallas_call(
        functools.partial(kernel, n, inner, prompt_rows),
        out_shape=shapes,
        in_specs=[hbm] * 9,
        out_specs=(hbm,) * 6,
        scratch_shapes=[
            pltpu.VMEM(query.shape, bf16),
            pltpu.VMEM(key.shape, bf16),
            pltpu.VMEM(key.shape, bf16),
            pltpu.VMEM(query.shape, bf16),
            pltpu.SMEM(lengths.shape, jnp.int32),
            pltpu.SMEM(lengths.shape, jnp.int32),
            pltpu.SMEM(lengths.shape, jnp.int32),
            pltpu.VMEM(prompt_key.shape, bf16),
            pltpu.VMEM(prompt_key.shape, bf16),
            *(pltpu.VMEM(shape.shape, bf16) for shape in shapes[2:]),
            pltpu.VMEM((n, 2, rows, width), bf16),
            pltpu.VMEM((n, rows, 2 * kv_width), bf16),
            pltpu.VMEM((slot, 2 * kv_width), bf16),
            pltpu.VMEM((outer, 2, inner * rows, width), bf16),
            pltpu.VMEM((outer, total, 2 * kv_width), bf16),
            pltpu.VMEM((n * slot, 2 * kv_width), bf16),
            pltpu.VMEM((outer, inner * rows, width), bf16),
            pltpu.VMEM((outer, inner * rows, width), bf16),
            pltpu.VMEM((outer, total, 2 * kv_width), bf16),
            pltpu.VMEM((n * slot, 2 * kv_width), bf16),
            pltpu.VMEM((outer, n, rows, 2 * kv_width), bf16),
            pltpu.VMEM((n, slot, 2 * kv_width), bf16),
            pltpu.VMEM((n * slot, 2 * kv_width), jnp.float32),
            dma((9,)), dma((2,)), dma((5,)), dma((outer,)), dma((outer,)),
            dma, dma((outer * (kv_width // HEAD_DIM),)), dma((outer, outer)), dma, dma, dma((outer,)), dma,
        ],
        compiler_params=pltpu.CompilerParams(
            collective_id=0, has_side_effects=True, vmem_limit_bytes=VMEM_BYTES
        ),
    )(*arrays)
    return pl.pallas_call(
        functools.partial(place_kernel, n),
        out_shape=shapes,
        in_specs=[hbm] * 7,
        out_specs=(hbm,) * 6,
        scratch_shapes=[
            *(pltpu.VMEM(shape.shape, bf16) for shape in shapes),
            pltpu.SMEM(home_rank.shape, jnp.int32),
            dma((6,)), dma((6,)), dma((n,)), dma,
        ],
        compiler_params=pltpu.CompilerParams(vmem_limit_bytes=VMEM_BYTES),
    )(*results, home_rank)


def body(*arrays):
    rows = arrays[0].shape[1]
    slot = -(-arrays[4].shape[0] // ROW_TILE) * ROW_TILE
    if rows % ROW_TILE == 0 and slot == rows and lax.axis_size("seq") % 2 == 0:
        return kernel_body(*arrays)
    return collective_body(*arrays)


def solution(mesh):
    placed = (
        P("group", "seq", "head"),
        P("group", "seq", "head"),
        P("group", "seq", "head"),
        P("group", "seq", "head"),
        P(("group", "seq"), "head"),
        P(("group", "seq"), "head"),
        P("group"),
        P("group"),
        P("group"),
    )
    return jax.shard_map(
        body,
        mesh=mesh,
        in_specs=placed,
        out_specs=(
            P(("group", "seq"), None, "head"),
            P("group", "seq", "head"),
            P("group", "seq", "head"),
            P("group", "seq", "head"),
            P(("group", "seq"), "head"),
            P(("group", "seq"), "head"),
        ),
        check_vma=False,
    )
```
